32 devices in a mesh: rows: 8 (over z, y), cols: 4 (over x, core).
Axes of the slice: x: 2, y: 2, z: 4, core: 2. Of those that a mesh axis runs over, the one named last changes fastest.
Arguments:
- features: float32 [8192, 4, 4, 256], P('rows', None, 'cols'), may hold values from -6 to 6
Outputs:
- factor_rows: float32 [512, 4, 4, 256], P(None, None, 'cols')
- basis: float32 [8192, 2, 256], P('rows')
- trailing: float32 [8192, 4, 4, 256], P('rows', None, 'cols')
The draws below stay inside these ranges and needn't reach their ends.
All inputs are finite; a program needn't handle non-finite values.
Results may differ from the reference program's by a relative error of at most 0.0003.
Values sent between devices are 32-bit elements; how exact they have to be, the bound alone decides.
No kernel may reach another device: no remote copies, remote signals or barrier semaphores. Data moves between devices by JAX's collectives and lax.ppermute only.
A program may use at most 64 MiB of HBM per device.

```python
import math
import jax
import jax.numpy as jnp
from jax import lax

PW = 256
PAN_DEV = 4
ROWS = 8192
N_COLS = 4


def draw_features(key, part):
    subkeys = jax.random.split(key, 4)
    full_shape = (ROWS, PAN_DEV, N_COLS, PW)
    row_shape = (ROWS, PAN_DEV, N_COLS, 1)
    column_shape = (1, PAN_DEV, N_COLS, PW)
    position = jnp.arange(ROWS, dtype=jnp.float32).reshape(ROWS, 1, 1, 1) / (ROWS - 1.0)
    noise = jnp.clip(jax.random.normal(subkeys[0], full_shape, jnp.float32), -4.0, 4.0)
    common = jnp.clip(jax.random.normal(subkeys[1], row_shape, jnp.float32), -4.0, 4.0)
    rising = jnp.exp(position * math.log(3.0)) * 0.6
    loading = jax.random.uniform(subkeys[2], column_shape, jnp.float32, 0.2, 0.6)
    spread = jax.random.uniform(subkeys[3], column_shape, jnp.float32, 0.5, 1.5)
    return jnp.clip(rising * (loading * common + spread * noise), -6.0, 6.0)


def setup_inputs(seed: int = 0) -> dict:
    streams_of = jax.random.split(jax.random.key(seed), 2)
    features = draw_features(jax.random.fold_in(streams_of[1], 71), 0)
    return dict(features=features)


def orthonormal(panel):
    qmat, rmat = jnp.linalg.qr(panel)
    signs = jnp.sign(jnp.diagonal(rmat))
    return qmat * signs[None, :]

def reference(features):
    matrix = features.reshape(ROWS, PAN_DEV * N_COLS * PW)
    basis_a = orthonormal(matrix[:, :PW])
    proj_a = jnp.dot(basis_a.T, matrix, precision=lax.Precision.HIGHEST)
    updated = matrix - jnp.dot(basis_a, proj_a, precision=lax.Precision.HIGHEST)
    basis_b = orthonormal(updated[:, PW:2 * PW])
    proj_b = jnp.dot(basis_b.T, updated, precision=lax.Precision.HIGHEST)
    final = updated - jnp.dot(basis_b, proj_b, precision=lax.Precision.HIGHEST)
    factor_rows = jnp.concatenate([proj_a, proj_b], axis=0).reshape(2 * PW, PAN_DEV, N_COLS, PW)
    basis = jnp.stack([basis_a, basis_b], axis=1)
    return (factor_rows, basis, final.reshape(ROWS, PAN_DEV, N_COLS, PW))
```

```python
import jax
import jax.numpy as jnp
from jax import lax
from jax.experimental import pallas as pl
from jax.experimental.pallas import tpu as pltpu
from jax.sharding import PartitionSpec as P

HIGHEST = lax.Precision.HIGHEST
LANES = 128
SUB = 8
F32 = jnp.float32
BF16 = jnp.bfloat16


def params(mib):
    return pltpu.CompilerParams(vmem_limit_bytes=mib * 1024 * 1024)


def vmem_spec():
    return pl.BlockSpec(memory_space=pltpu.VMEM)


def smem_spec():
    return pl.BlockSpec(memory_space=pltpu.SMEM)


def split(value):
    high = value.astype(BF16)
    return high, (value - high.astype(F32)).astype(BF16)


NN = (((1,), (0,)), ((), ()))
NT = (((1,), (1,)), ((), ()))


def dot3(left, right, dims=NN):
    def one(a, b):
        return lax.dot_general(a, b, dims, preferred_element_type=F32)

    return one(left[0], right[0]) + (one(left[0], right[1]) + one(left[1], right[0]))


def panel_kernel(x_ref, out_ref):
    rows = out_ref.shape[1]
    blocks = x_ref.shape[0] // rows
    for half in range(out_ref.shape[0]):
        out_ref[half] = x_ref[pl.ds(half, rows, stride=blocks), :]


def own_panel(lines, rows, blocks, halves):
    step = 256
    return pl.pallas_call(
        panel_kernel,
        grid=(rows // step,),
        in_specs=[pl.BlockSpec((step * blocks, LANES), lambda i: (i, 0))],
        out_specs=pl.BlockSpec((halves, step, LANES), lambda i: (0, i, 0)),
        out_shape=jax.ShapeDtypeStruct((halves, rows, LANES), F32),
        name="own_panel",
    )(lines)


def gram_kernel(core_ref, a_ref, b_ref, out_ref):
    core = core_ref[0]

    def pick(zero, one):
        return jnp.where(core == 0, zero, one)

    own = jnp.concatenate([a_ref[0], a_ref[1]], axis=1)
    other = jnp.concatenate([b_ref[0], b_ref[1]], axis=1)
    first = pick(own, other)
    cross = pick(b_ref[0], a_ref[1])
    left = split(jnp.concatenate([own.T, cross.T], axis=0))
    right_own = split(own)
    right_first = split(first)
    width = own.shape[1]
    left_own = tuple(part[:width] for part in left)
    left_cross = tuple(part[width:] for part in left)
    mine = dot3(left_own, right_own)
    mixed = dot3(left_cross, right_first)
    out_ref[0] = mine[:LANES, :LANES]
    out_ref[1] = mine[LANES:, :LANES]
    out_ref[2] = mine[LANES:, LANES:]
    out_ref[3] = mixed[:, :LANES]
    out_ref[4] = mixed[:, LANES:]


def panel_gram(core, own, other):
    return pl.pallas_call(
        gram_kernel,
        in_specs=[smem_spec(), vmem_spec(), vmem_spec()],
        out_specs=vmem_spec(),
        out_shape=jax.ShapeDtypeStruct((5, LANES, LANES), F32),
        compiler_params=params(48),
        name="panel_gram",
    )(core, own, other)


def product_kernel(base_ref, x_ref, p0_ref, p1_ref, out_ref):
    rows = p0_ref.shape[0]
    blocks = x_ref.shape[0] // rows
    count = out_ref.shape[0]
    base = base_ref[0]
    left = split(jnp.concatenate([p0_ref[...].T, p1_ref[...].T], axis=0))
    parts = [x_ref[pl.ds(base + i, rows, stride=blocks), :] for i in range(count)]
    result = dot3(left, split(jnp.concatenate(parts, axis=1)))
    for i in range(count):
        out_ref[i] = result[:, i * LANES:(i + 1) * LANES]


def panel_products(base, lines, p0, p1, count):
    return pl.pallas_call(
        product_kernel,
        in_specs=[smem_spec(), vmem_spec(), vmem_spec(), vmem_spec()],
        out_specs=vmem_spec(),
        out_shape=jax.ShapeDtypeStruct((count, 2 * LANES, LANES), F32),
        compiler_params=params(48),
        name="panel_products",
    )(base, lines, p0, p1)


def lane_copy(value, lane):
    return jnp.broadcast_to(value[:, lane:lane + 1], value.shape)


def row_copy(value, row):
    return jnp.broadcast_to(value[row:row + 1, :], value.shape)


def inverse_factor(block):
    groups = LANES // SUB
    lane = lax.broadcasted_iota(jnp.int32, (SUB, LANES), 1)
    sub = lax.broadcasted_iota(jnp.int32, (SUB, LANES), 0)
    work = [block[SUB * g:SUB * (g + 1), :] for g in range(groups)]
    result = []
    for g in range(groups):
        start = SUB * g
        panel = work[g]
        inside = (lane >= start) & (lane < start + SUB)
        cols = [lane_copy(panel, start + j) for j in range(SUB)]
        c = {(s, j): row_copy(cols[j], s) for j in range(SUB) for s in range(j, SUB)}
        mult, recip = {}, []
        for i in range(SUB):
            recip.append(1.0 / c[i, i])
            for s in range(i + 1, SUB):
                mult[s, i] = c[s, i] * recip[i]
                for t in range(i + 1, s + 1):
                    c[s, t] = c[s, t] - mult[s, i] * c[t, i]
        unit = jnp.where(inside, jnp.where(lane == start + sub, 1.0, 0.0), panel)
        upper = []
        for s in range(SUB):
            row = row_copy(unit, s)
            for i in range(s):
                row = row - mult[s, i] * upper[i]
            upper.append(row)
        solved = [None] * SUB
        for s in reversed(range(SUB)):
            row = upper[s] * recip[s]
            for t in range(s + 1, SUB):
                row = row - mult[t, s] * solved[t]
            solved[s] = row
        for later in range(g + 1, groups):
            old = work[later]
            new = jnp.where(inside, 0.0, old)
            for j in range(SUB):
                new = new - lane_copy(old, start + j) * solved[j]
            work[later] = new
        rows = upper[0]
        diag = c[0, 0]
        for s in range(1, SUB):
            rows = jnp.where(sub == s, upper[s], rows)
            diag = jnp.where(sub == s, c[s, s], diag)
        result.append(jnp.where(lane < start + SUB, rows * lax.rsqrt(diag), 0.0))
    return jnp.concatenate(result, axis=0)


def dot6(a, b, dims=NN):
    return lax.dot_general(a, b, dims, precision=HIGHEST, preferred_element_type=F32)


def factor_kernel(g0_ref, g1_ref, out_ref):
    s = {
        (0, 0): g0_ref[0], (1, 0): g0_ref[1], (1, 1): g0_ref[2],
        (2, 0): g0_ref[3], (2, 1): g0_ref[4],
        (2, 2): g1_ref[0], (3, 2): g1_ref[1], (3, 3): g1_ref[2],
        (3, 0): g1_ref[3], (3, 1): g1_ref[4],
    }
    n = 4
    e = {}
    for k in range(n):
        m = inverse_factor(s[k, k])
        x = {j: dot6(m, e[k, j]) for j in range(k)}
        x[k] = m
        for j in range(n):
            value = x[j] if j <= k else jnp.zeros((LANES, LANES), F32)
            out_ref[k * LANES:(k + 1) * LANES, j * LANES:(j + 1) * LANES] = value
        low = {i: dot6(s[i, k], m, NT) for i in range(k + 1, n)}
        for i in range(k + 1, n):
            for j in range(k + 1, i + 1):
                s[i, j] = s[i, j] - dot6(low[i], low[j], NT)
            for j in range(k + 1):
                term = dot6(low[i], x[j])
                e[i, j] = e[i, j] - term if (i, j) in e else -term


def inverse_of_factor(g0, g1):
    size = 4 * LANES
    return pl.pallas_call(
        factor_kernel,
        in_specs=[vmem_spec(), vmem_spec()],
        out_specs=vmem_spec(),
        out_shape=jax.ShapeDtypeStruct((size, size), F32),
        compiler_params=params(48),
        name="inverse_of_factor",
    )(g0, g1)


def basis_kernel(a0_ref, a1_ref, x_ref, lines_ref, high_ref, low_ref):
    rows = a0_ref.shape[1]
    panels = jnp.concatenate([a0_ref[0], a0_ref[1], a1_ref[0], a1_ref[1]], axis=1)
    q = dot3(split(panels), split(x_ref[...]), NT)
    high, low = split(q)
    high_ref[...] = high
    low_ref[...] = low
    for panel in range(2):
        for half in range(2):
            k = 2 * panel + half
            lines_ref[pl.ds(2 * half + panel, rows, stride=4), :] = q[:, k * LANES:(k + 1) * LANES]


def panel_bases(a0, a1, inverse):
    halves, rows, lanes = a0.shape
    size = inverse.shape[0]
    step = 256
    return pl.pallas_call(
        basis_kernel,
        grid=(rows // step,),
        in_specs=[
            pl.BlockSpec((halves, step, lanes), lambda i: (0, i, 0)),
            pl.BlockSpec((halves, step, lanes), lambda i: (0, i, 0)),
            pl.BlockSpec((size, size), lambda i: (0, 0)),
        ],
        out_specs=[
            pl.BlockSpec((4 * step, lanes), lambda i: (i, 0)),
            pl.BlockSpec((step, size), lambda i: (i, 0)),
            pl.BlockSpec((step, size), lambda i: (i, 0)),
        ],
        out_shape=[
            jax.ShapeDtypeStruct((4 * rows, lanes), F32),
            jax.ShapeDtypeStruct((rows, size), BF16),
            jax.ShapeDtypeStruct((rows, size), BF16),
        ],
        compiler_params=params(48),
        name="panel_bases",
    )(a0, a1, inverse)


def trailing_kernel(bases_ref, x_ref, qh_ref, ql_ref, inv_ref, m0_ref, m1_ref, r0_ref, r1_ref,
                    factor_ref, out_ref, wh_ref, wl_ref):
    rows = qh_ref.shape[0]
    blocks = x_ref.shape[0] // rows
    count = m0_ref.shape[0]
    size = inv_ref.shape[0]

    @pl.when(pl.program_id(0) == 0)
    def _():
        inverse = split(inv_ref[...])
        for side, (h0, h1) in enumerate(((m0_ref, m1_ref), (r0_ref, r1_ref))):
            columns = []
            for i in range(count):
                columns.append(jnp.concatenate(
                    [h0[i, :LANES], h1[i, :LANES], h0[i, LANES:], h1[i, LANES:]], axis=0))
            w = dot3(inverse, split(jnp.concatenate(columns, axis=1)))
            for i in range(count):
                factor_ref[pl.ds(bases_ref[side] + i, size, stride=blocks), :] = (
                    w[:, i * LANES:(i + 1) * LANES])
            high, low = split(w)
            wh_ref[side] = high
            wl_ref[side] = low

    q = (qh_ref[...], ql_ref[...])
    for side in range(2):
        term = dot3(q, (wh_ref[side], wl_ref[side]))
        for i in range(count):
            where = pl.ds(bases_ref[side] + i, rows, stride=blocks)
            out_ref[where, :] = x_ref[where, :] - term[:, i * LANES:(i + 1) * LANES]


def finish(bases, lines, q_high, q_low, inverse, mine, received):
    rows, size = q_high.shape
    blocks = lines.shape[0] // rows
    count = mine[0].shape[0]
    step = 256
    whole = pl.BlockSpec((count, 2 * LANES, LANES), lambda i: (0, 0, 0))
    return pl.pallas_call(
        trailing_kernel,
        grid=(rows // step,),
        in_specs=[
            smem_spec(),
            pl.BlockSpec((step * blocks, LANES), lambda i: (i, 0)),
            pl.BlockSpec((step, size), lambda i: (i, 0)),
            pl.BlockSpec((step, size), lambda i: (i, 0)),
            pl.BlockSpec((size, size), lambda i: (0, 0)),
            whole, whole, whole, whole,
        ],
        out_specs=[
            pl.BlockSpec((size * blocks, LANES), lambda i: (0, 0)),
            pl.BlockSpec((step * blocks, LANES), lambda i: (i, 0)),
        ],
        out_shape=[
            jax.ShapeDtypeStruct((size * blocks, LANES), F32),
            jax.ShapeDtypeStruct(lines.shape, F32),
        ],
        scratch_shapes=[
            pltpu.VMEM((2, size, count * LANES), BF16),
            pltpu.VMEM((2, size, count * LANES), BF16),
        ],
        compiler_params=params(56),
        name="finish",
    )(bases, lines, q_high, q_low, inverse, mine[0], mine[1], received[0], received[1])


def swap(value, axis, size, bit):
    return lax.ppermute(value, axis, [(i, i ^ bit) for i in range(size)])


def spread(value, col, cols):
    span = 2
    while span < cols:
        got = lax.ppermute(value, "cols", [(i, i + span) for i in range(min(span, cols - span))])
        value = jnp.where(col < span, value, got)
        span *= 2
    return value


def bits_of(size):
    bits, bit = [], 1
    while bit < size:
        bits.append(bit)
        bit *= 2
    return bits


def halves_of(value, flag):
    half = value.shape[0] // 2
    keep = lax.dynamic_slice_in_dim(value, flag * half, half, 0)
    give = lax.dynamic_slice_in_dim(value, (1 - flag) * half, half, 0)
    return keep, give


def join(mine, got, flag):
    return jnp.where(flag == 0, jnp.concatenate([mine, got], 0), jnp.concatenate([got, mine], 0))


def sum_rows(mine, got, row, rows):
    shape = mine.shape
    value = (mine + got).reshape(-1, shape[-1])
    bits = bits_of(rows)[1:]
    for bit in bits:
        keep, give = halves_of(value, (row // bit) % 2)
        value = keep + swap(give, "rows", rows, bit)
    for bit in reversed(bits):
        value = join(value, swap(value, "rows", rows, bit), (row // bit) % 2)
    return value.reshape(shape)


def program(rows_n, cols_n):
    def on_device(features):
        rows, panels, _, width = features.shape
        halves = width // LANES
        blocks = panels * halves
        lines = features.reshape(rows * blocks, LANES)
        row, col = lax.axis_index("rows"), lax.axis_index("cols")
        core = col % 2
        own = own_panel(lines, rows, blocks, halves)

        other = swap(own, "cols", cols_n, 1)
        gram = panel_gram(core.reshape(1), own, other)
        gram = gram.reshape(-1, LANES)
        keep, give = halves_of(gram, row % 2)
        gram = keep + swap(give, "rows", rows_n, 1)
        for bit in bits_of(rows_n)[1:]:
            gram = gram + swap(gram, "rows", rows_n, bit)
        gram = join(gram, swap(gram, "rows", rows_n, 1), row % 2)
        gram = spread(gram, col, cols_n)
        got = swap(gram, "cols", cols_n, 1)
        shape = (5, LANES, LANES)
        first = jnp.where(core == 0, gram, got).reshape(shape)
        second = jnp.where(core == 0, got, gram).reshape(shape)
        inverse = inverse_of_factor(first, second)

        count = blocks // 2
        near = (row % 2) * count
        far = count - near
        mine, received, p0, p1 = [], [], [], []
        for half in range(halves):
            piece = spread(own[half], col, cols_n)
            twin = swap(piece, "cols", cols_n, 1)
            zero = jnp.where(core == 0, piece, twin)
            one = jnp.where(core == 0, twin, piece)
            p0.append(zero)
            p1.append(one)
            give = panel_products(far.reshape(1), lines, zero, one, count)
            keep = panel_products(near.reshape(1), lines, zero, one, count)
            total = sum_rows(keep, swap(give, "rows", rows_n, 1), row, rows_n)
            mine.append(total)
            received.append(swap(total, "rows", rows_n, 1))

        a0, a1 = jnp.stack(p0), jnp.stack(p1)
        basis, q_high, q_low = panel_bases(a0, a1, inverse)
        factor, trailing = finish(jnp.stack([near, far]), lines, q_high, q_low, inverse, mine, received)
        basis = basis.reshape(rows, halves, 2, LANES).transpose(0, 2, 1, 3).reshape(rows, 2, width)
        return (factor.reshape(2 * width, panels, 1, width), basis, trailing.reshape(features.shape))

    return on_device


def solution(mesh):
    placed = (P("rows", None, "cols", None),)
    return jax.shard_map(
        program(mesh.shape["rows"], mesh.shape["cols"]),
        mesh=mesh,
        in_specs=placed,
        out_specs=(
            P(None, None, "cols", None),
            P("rows", None, None),
            P("rows", None, "cols", None),
        ),
        check_vma=False,
    )
```

```python
import functools

import jax
import jax.numpy as jnp
from jax import lax
from jax.experimental import pallas as pl
from jax.experimental.pallas import tpu as pltpu
from jax.sharding import PartitionSpec as P

HIGHEST = lax.Precision.HIGHEST
LANES = 128
SUB = 8
F32 = jnp.float32
BF16 = jnp.bfloat16


def params():
    return pltpu.CompilerParams(vmem_limit_bytes=48 * 1024 * 1024)


def vmem_spec():
    return pl.BlockSpec(memory_space=pltpu.VMEM)


def smem_spec():
    return pl.BlockSpec(memory_space=pltpu.SMEM)


def split(value):
    high = value.astype(BF16)
    return high, (value - high.astype(F32)).astype(BF16)


NN = (((1,), (0,)), ((), ()))
NT = (((1,), (1,)), ((), ()))


def dot3(left, right, dims=NN):
    def one(a, b):
        return lax.dot_general(a, b, dims, preferred_element_type=F32)

    return one(left[0], right[0]) + (one(left[0], right[1]) + one(left[1], right[0]))


def panel_kernel(x_ref, *refs):
    slabs, both, sems = refs[:-2], refs[-2], refs[-1]
    copies = [
        pltpu.make_async_copy(x_ref.at[:, 0, half], both.at[half], sems.at[half])
        for half in range(len(slabs))
    ]
    for copy in copies:
        copy.start()
    for half, slab in enumerate(slabs):
        copies[half].wait()
        slab[...] = both[half]


def own_panel(features):
    rows, panels, _, width = features.shape
    halves = width // LANES
    slab = jax.ShapeDtypeStruct((rows, LANES), F32)
    *slabs, both = pl.pallas_call(
        panel_kernel,
        in_specs=[pl.BlockSpec(memory_space=pltpu.HBM)],
        out_specs=[vmem_spec()] * (halves + 1),
        out_shape=[slab] * halves + [jax.ShapeDtypeStruct((halves, rows, LANES), F32)],
        scratch_shapes=[pltpu.SemaphoreType.DMA((halves,))],
        compiler_params=params(),
        cost_estimate=cost(2),
        name="own_panel",
    )(features.reshape(rows, panels, halves, LANES))
    return slabs, both


def any_spec():
    return pl.BlockSpec(memory_space=pl.ANY)


def cost(micros=0):
    return pl.CostEstimate(flops=1 + micros * 10 ** 9, bytes_accessed=1, transcendentals=0)


def held_kernel(value_ref, *refs):
    del value_ref, refs


def held(value, *after):
    return pl.pallas_call(
        held_kernel,
        in_specs=[any_spec()] * (1 + len(after)),
        out_specs=any_spec(),
        out_shape=jax.ShapeDtypeStruct(value.shape, value.dtype),
        input_output_aliases={0: 0},
        compiler_params=params(),
        cost_estimate=cost(),
        name="held",
    )(value, *after)


def halve_kernel(flag_ref, mine_ref, got_ref, *refs):
    keep_ref, give_ref = refs[-2:]
    half = keep_ref.shape[0]
    near = pl.multiple_of(flag_ref[0] * half, half)
    far = pl.multiple_of((1 - flag_ref[0]) * half, half)
    give_ref[...] = mine_ref[pl.ds(far, half), :] + got_ref[pl.ds(far, half), :]
    keep_ref[...] = mine_ref[pl.ds(near, half), :] + got_ref[pl.ds(near, half), :]


def halve(mine, got, flag, *after):
    rows, lanes = mine.shape
    half = jax.ShapeDtypeStruct((rows // 2, lanes), F32)
    return pl.pallas_call(
        halve_kernel,
        in_specs=[smem_spec()] + [vmem_spec()] * 2 + [any_spec()] * len(after),
        out_specs=[vmem_spec()] * 2,
        out_shape=[half, half],
        compiler_params=params(),
        cost_estimate=cost(),
        name="halve",
    )(flag.reshape(1), mine, got, *after)


def add_kernel(mine_ref, got_ref, *refs):
    refs[-1][...] = mine_ref[...] + got_ref[...]


def add(mine, got, *after):
    return pl.pallas_call(
        add_kernel,
        in_specs=[vmem_spec()] * 2 + [any_spec()] * len(after),
        out_specs=vmem_spec(),
        out_shape=jax.ShapeDtypeStruct(mine.shape, F32),
        compiler_params=params(),
        cost_estimate=cost(),
        name="add",
    )(mine, got, *after)


def join_kernel(flag_ref, mine_ref, got_ref, *refs):
    out_ref = refs[-1]
    half = mine_ref.shape[0]
    out_ref[pl.ds(pl.multiple_of(flag_ref[0] * half, half), half), :] = mine_ref[...]
    out_ref[pl.ds(pl.multiple_of((1 - flag_ref[0]) * half, half), half), :] = got_ref[...]


def join(mine, got, flag, *after):
    rows, lanes = mine.shape
    return pl.pallas_call(
        join_kernel,
        in_specs=[smem_spec()] + [vmem_spec()] * 2 + [any_spec()] * len(after),
        out_specs=vmem_spec(),
        out_shape=jax.ShapeDtypeStruct((2 * rows, lanes), F32),
        compiler_params=params(),
        cost_estimate=cost(),
        name="join",
    )(flag.reshape(1), mine, got, *after)


def gram_kernel(flags_ref, a_ref, b_ref, keep_ref, give_ref, work_ref):
    flag, core = flags_ref[0], flags_ref[1]

    def pick(zero, one):
        return jnp.where(core == 0, zero, one)

    own = jnp.concatenate([a_ref[0], a_ref[1]], axis=1)
    other = jnp.concatenate([b_ref[0], b_ref[1]], axis=1)
    first = pick(own, other)
    cross = pick(b_ref[0], a_ref[1])
    left = split(jnp.concatenate([own.T, cross.T], axis=0))
    width = own.shape[1]
    mine = dot3(tuple(part[:width] for part in left), split(own))
    mixed = dot3(tuple(part[width:] for part in left), split(first))
    parts = [mine[:LANES, :LANES], mine[LANES:, :LANES], mine[LANES:, LANES:],
             mixed[:, :LANES], mixed[:, LANES:]]
    for i, part in enumerate(parts):
        work_ref[i * LANES:(i + 1) * LANES, :] = part
    half = keep_ref.shape[0]
    keep_ref[...] = work_ref[pl.ds(pl.multiple_of(flag * half, half), half), :]
    give_ref[...] = work_ref[pl.ds(pl.multiple_of((1 - flag) * half, half), half), :]


def panel_gram(flags, own, other):
    half = jax.ShapeDtypeStruct((5 * LANES // 2, LANES), F32)
    return pl.pallas_call(
        gram_kernel,
        in_specs=[smem_spec(), vmem_spec(), vmem_spec()],
        out_specs=[vmem_spec()] * 2,
        out_shape=[half, half],
        scratch_shapes=[pltpu.VMEM((5 * LANES, LANES), F32)],
        compiler_params=params(),
        cost_estimate=cost(1),
        name="panel_gram",
    )(flags, own, other)


def fetch(x_ref, first, slabs_ref, sems):
    copies = []
    for i in range(slabs_ref.shape[0]):
        halves = x_ref.shape[2]
        source = x_ref.at[:, first + i // halves, i % halves]
        copies.append(pltpu.make_async_copy(source, slabs_ref.at[i], sems.at[i]))
    for copy in copies:
        copy.start()
    return copies


def times_columns(left, copies, slabs_ref, out_ref):
    for copy in copies:
        copy.wait()
    right = jnp.concatenate([slabs_ref[i] for i in range(slabs_ref.shape[0])], axis=1)
    value = dot3(left, split(right))
    height = value.shape[0]
    for i in range(slabs_ref.shape[0]):
        out_ref[i * height:(i + 1) * height, :] = value[:, i * LANES:(i + 1) * LANES]


def choose(flags_ref, own, other, got, twin):
    mine = jnp.where(flags_ref[2] == 1, own, got)
    paired = jnp.where(flags_ref[2] == 1, other, twin)
    zero = jnp.where(flags_ref[1] == 0, mine, paired)
    one = jnp.where(flags_ref[1] == 0, paired, mine)
    return zero, one


def product_kernel(flags_ref, x_ref, own_ref, other_ref, got_ref, twin_ref, *refs):
    give_ref, keep_ref, far_ref, near_ref, sems = refs[-5:]
    panels = x_ref.shape[1] // 2
    far = fetch(x_ref, (1 - flags_ref[0]) * panels, far_ref, sems.at[0])
    near = fetch(x_ref, flags_ref[0] * panels, near_ref, sems.at[1])
    zero, one = choose(flags_ref, own_ref[...], other_ref[...], got_ref[...], twin_ref[...])
    left = split(jnp.concatenate([zero, one], axis=1).T)
    times_columns(left, far, far_ref, give_ref)
    times_columns(left, near, near_ref, keep_ref)


def panel_products(flags, features, own, other, got, twin, *after):
    rows, panels, _, width = features.shape
    count = panels * width // LANES // 2
    x = features.reshape(rows, panels, width // LANES, LANES)
    out = jax.ShapeDtypeStruct((count * 2 * LANES, LANES), F32)
    return pl.pallas_call(
        product_kernel,
        in_specs=[smem_spec(), pl.BlockSpec(memory_space=pltpu.HBM)]
        + [vmem_spec()] * 4 + [any_spec()] * len(after),
        out_specs=[vmem_spec()] * 2,
        out_shape=[out, out],
        scratch_shapes=[pltpu.VMEM((count, rows, LANES), F32)] * 2
        + [pltpu.SemaphoreType.DMA((2, count))],
        compiler_params=params(),
        cost_estimate=cost(4),
        name="panel_products",
    )(flags, x, own, other, got, twin, *after)


def lane_copy(value, lane):
    return jnp.broadcast_to(value[:, lane:lane + 1], value.shape)


def row_copy(value, row):
    return jnp.broadcast_to(value[row:row + 1, :], value.shape)


def inverse_factor(block):
    groups = LANES // SUB
    lane = lax.broadcasted_iota(jnp.int32, (SUB, LANES), 1)
    sub = lax.broadcasted_iota(jnp.int32, (SUB, LANES), 0)
    work = [block[SUB * g:SUB * (g + 1), :] for g in range(groups)]
    result = []
    for g in range(groups):
        start = SUB * g
        panel = work[g]
        inside = (lane >= start) & (lane < start + SUB)
        cols = [lane_copy(panel, start + j) for j in range(SUB)]
        c = {(s, j): row_copy(cols[j], s) for j in range(SUB) for s in range(j, SUB)}
        mult, recip, diag = {}, [], []
        for i in range(0, SUB, 2):
            a, b, d = c[i, i], c[i + 1, i], c[i + 1, i + 1]
            det = a * d - b * b
            ra, rdet = 1.0 / a, 1.0 / det
            f = b * ra
            mult[i + 1, i] = f
            rb = a * rdet
            recip += [ra, rb]
            diag += [a, det * ra]
            for s in range(i + 2, SUB):
                mult[s, i] = c[s, i] * ra
                c[s, i + 1] = c[s, i + 1] - f * c[s, i]
                mult[s, i + 1] = c[s, i + 1] * rb
            for s in range(i + 2, SUB):
                for t in range(i + 2, s + 1):
                    c[s, t] = (c[s, t] - mult[s, i] * c[t, i]) - mult[s, i + 1] * c[t, i + 1]
        unit = jnp.where(inside, jnp.where(lane == start + sub, 1.0, 0.0), panel)
        upper = []
        for s in range(SUB):
            row = row_copy(unit, s)
            for i in range(s):
                row = row - mult[s, i] * upper[i]
            upper.append(row)
        scaled = [upper[s] * recip[s] for s in range(SUB)]
        nxt = g + 1
        if nxt < groups:
            old = work[nxt]
            new = jnp.where(inside, 0.0, old)
            v = []
            for j in range(SUB):
                e = lane_copy(old, start + j)
                for i in range(j):
                    e = e - mult[j, i] * v[i]
                v.append(e)
                new = new - e * scaled[j]
            work[nxt] = new
            nxt += 1
        if nxt < groups:
            solved = [None] * SUB
            for s in reversed(range(SUB)):
                row = scaled[s]
                for t in reversed(range(s + 1, SUB)):
                    row = row - mult[t, s] * solved[t]
                solved[s] = row
        for later in range(nxt, groups):
            old = work[later]
            new = jnp.where(inside, 0.0, old)
            for j in range(SUB):
                new = new - lane_copy(old, start + j) * solved[j]
            work[later] = new
        rows, dg = upper[0], diag[0]
        for s in range(1, SUB):
            rows = jnp.where(sub == s, upper[s], rows)
            dg = jnp.where(sub == s, diag[s], dg)
        result.append(jnp.where(lane < start + SUB, rows * lax.rsqrt(dg), 0.0))
    return jnp.concatenate(result, axis=0)


def dot6(a, b, dims=NN):
    return lax.dot_general(a, b, dims, precision=HIGHEST, preferred_element_type=F32)


STAGES = 4


def place(i, j):
    return i * (i + 1) // 2 + j


def stage(k, s):
    m = inverse_factor(s[k, k])
    for j in range(k):
        s[k, j] = dot6(m, s[k, j])
    low = {i: dot6(s[i, k], m, NT) for i in range(k + 1, STAGES)}
    s[k, k] = m
    for i in range(k + 1, STAGES):
        for j in range(k + 1, i + 1):
            s[i, j] = s[i, j] - dot6(low[i], low[j], NT)
        for j in range(k):
            s[i, j] = s[i, j] - dot6(low[i], s[k, j])
        s[i, k] = -dot6(low[i], m)


def first_stage_kernel(core_ref, mine_ref, twin_ref, *refs):
    out_ref = refs[-1]
    zero = jnp.where(core_ref[0] == 0, mine_ref[...], twin_ref[...])
    one = jnp.where(core_ref[0] == 0, twin_ref[...], mine_ref[...])

    def block(value, i):
        return value[i * LANES:(i + 1) * LANES]

    s = {
        (0, 0): block(zero, 0), (1, 0): block(zero, 1), (1, 1): block(zero, 2),
        (2, 0): block(zero, 3), (2, 1): block(zero, 4),
        (2, 2): block(one, 0), (3, 2): block(one, 1), (3, 3): block(one, 2),
        (3, 0): block(one, 3), (3, 1): block(one, 4),
    }
    stage(0, s)
    for (i, j), value in s.items():
        out_ref[place(i, j)] = value


def later_stage_kernel(k, in_ref, *refs):
    s = {(i, j): in_ref[place(i, j)] for i in range(STAGES) for j in range(i + 1)}
    stage(k, s)
    for (i, j), value in s.items():
        refs[-1][place(i, j)] = value


def stage_call(kernel, name, operands, scalars, after):
    return pl.pallas_call(
        kernel,
        in_specs=[smem_spec()] * scalars + [vmem_spec()] * (len(operands) - scalars)
        + [any_spec()] * len(after),
        out_specs=vmem_spec(),
        out_shape=jax.ShapeDtypeStruct((place(STAGES, 0), LANES, LANES), F32),
        compiler_params=params(),
        cost_estimate=cost(5),
        name=name,
    )(*operands, *after)


def first_stage(core, mine, twin, *after):
    return stage_call(first_stage_kernel, "factor_0", [core.reshape(1), mine, twin], 1, after)


def later_stage(k, state, *after):
    return stage_call(functools.partial(later_stage_kernel, k), "factor_%d" % k, [state], 0, after)


def packed(ref):
    zero = jnp.zeros((LANES, LANES), F32)
    rows = [
        jnp.concatenate([ref[place(i, j)] if j <= i else zero for j in range(STAGES)], axis=1)
        for i in range(STAGES)
    ]
    return jnp.concatenate(rows, axis=0)


def basis_kernel(flags_ref, *refs):
    halves = (len(refs) - 4) // 4
    x_ref, lines_ref, high_ref, low_ref = refs[-4:]
    zeros, ones = [], []
    for half in range(halves):
        zero, one = choose(flags_ref, *(ref[...] for ref in refs[4 * half:4 * half + 4]))
        zeros.append(zero)
        ones.append(one)
    rows = zeros[0].shape[0]
    panels = jnp.concatenate(zeros + ones, axis=1)
    q = dot3(split(panels), split(packed(x_ref)), NT)
    high, low = split(q)
    high_ref[...] = high
    low_ref[...] = low
    for panel in range(2):
        for half in range(2):
            k = 2 * panel + half
            lines_ref[pl.ds(2 * half + panel, rows, stride=4), :] = q[:, k * LANES:(k + 1) * LANES]


def panel_bases(flags, slabs, inverse):
    rows = slabs[0].shape[0]
    size = STAGES * LANES
    step = 256
    piece = pl.BlockSpec((step, LANES), lambda i: (i, 0))
    wide = pl.BlockSpec((step, size), lambda i: (i, 0))
    return pl.pallas_call(
        basis_kernel,
        grid=(rows // step,),
        in_specs=[smem_spec()] + [piece] * len(slabs) + [vmem_spec()],
        out_specs=[pl.BlockSpec((4 * step, LANES), lambda i: (i, 0)), wide, wide],
        out_shape=[
            jax.ShapeDtypeStruct((4 * rows, LANES), F32),
            jax.ShapeDtypeStruct((rows, size), BF16),
            jax.ShapeDtypeStruct((rows, size), BF16),
        ],
        compiler_params=params(),
        cost_estimate=cost(5),
        name="panel_bases",
    )(flags, *slabs, inverse)


def trailing_kernel(flags_ref, x_ref, qh_ref, ql_ref, inv_ref, h0_ref, h1_ref, *refs):
    factor_ref, out_ref, x_slabs, w_slabs, out_slabs, x_sems, w_sems, out_sems = refs[-8:]
    count, rows = x_slabs.shape[0], x_slabs.shape[1]
    halves = x_ref.shape[2]
    first = flags_ref[0] * x_ref.shape[1] // 2
    fetched = fetch(x_ref, first, x_slabs, x_sems)
    columns = []
    for i in range(count):
        at = [(2 * i + p) * LANES for p in range(2)]
        columns.append(jnp.concatenate([ref[a:a + LANES] for a in at for ref in (h0_ref, h1_ref)], axis=0))
    w = dot3(split(packed(inv_ref)), split(jnp.concatenate(columns, axis=1)))
    sent = []
    for i in range(count):
        w_slabs[i] = w[:, i * LANES:(i + 1) * LANES]
        target = factor_ref.at[:, first + i // halves, i % halves]
        sent.append(pltpu.make_async_copy(w_slabs.at[i], target, w_sems.at[i]))
        sent[-1].start()
    right = split(w)
    for copy in fetched:
        copy.wait()
    chunks = out_sems.shape[0]
    step = rows // chunks
    for chunk in range(chunks):
        here = pl.ds(chunk * step, step)
        term = dot3((qh_ref[here, :], ql_ref[here, :]), right)
        for i in range(count):
            out_slabs[i, here, :] = x_slabs[i, here, :] - term[:, i * LANES:(i + 1) * LANES]
            target = out_ref.at[here, first + i // halves, i % halves]
            sent.append(pltpu.make_async_copy(out_slabs.at[i, here], target, out_sems.at[chunk, i]))
            sent[-1].start()
    for copy in sent:
        copy.wait()


def finish(side, features, q_high, q_low, inverse, pieces, outs, *after):
    rows, panels, _, width = features.shape
    halves = width // LANES
    size = q_high.shape[1]
    count = panels * halves // 2
    x = features.reshape(rows, panels, halves, LANES)
    hbm = pl.BlockSpec(memory_space=pltpu.HBM)
    chunks = 4
    extra = len(outs)
    return pl.pallas_call(
        trailing_kernel,
        in_specs=[smem_spec(), hbm] + [vmem_spec()] * 5 + [hbm] * extra + [any_spec()] * len(after),
        out_specs=[hbm, hbm],
        out_shape=[
            jax.ShapeDtypeStruct((size, panels, halves, LANES), F32),
            jax.ShapeDtypeStruct(x.shape, F32),
        ],
        scratch_shapes=[
            pltpu.VMEM((count, rows, LANES), F32),
            pltpu.VMEM((count, size, LANES), F32),
            pltpu.VMEM((count, rows, LANES), F32),
            pltpu.SemaphoreType.DMA((count,)),
            pltpu.SemaphoreType.DMA((count,)),
            pltpu.SemaphoreType.DMA((chunks, count)),
        ],
        input_output_aliases={7 + i: i for i in range(extra)},
        compiler_params=params(),
        cost_estimate=cost(5),
        name="finish",
    )(side.reshape(1), x, q_high, q_low, inverse, *pieces, *outs, *after)


def swap(value, axis, size, bit):
    return lax.ppermute(value, axis, [(i, i ^ bit) for i in range(size)])


def spread(value, col, cols):
    got, span = None, 2
    while span < cols:
        new = lax.ppermute(value, "cols", [(i, i + span) for i in range(min(span, cols - span))])
        got = new if got is None else jnp.where(col < span, got, new)
        span *= 2
        if span < cols:
            value = jnp.where(col < 2, value, got)
    return got


def bits_of(size):
    bits, bit = [], 1
    while bit < size:
        bits.append(bit)
        bit *= 2
    return bits


def sum_steps(mine, got, row, rows):
    bits = bits_of(rows)[1:]
    after = yield
    for bit in bits:
        mine, give = halve(mine, got, (row // bit) % 2, after)
        got = swap(give, "rows", rows, bit)
        after = yield mine
    value = add(mine, got, after)
    for bit in reversed(bits):
        got = swap(value, "rows", rows, bit)
        after = yield value
        value = join(value, got, (row // bit) % 2, after)
    yield value


def program(rows_n, cols_n):
    bits = bits_of(rows_n)[1:]

    def on_device(features):
        rows, panels, _, width = features.shape
        halves = width // LANES
        row, col = lax.axis_index("rows"), lax.axis_index("cols")
        side, core, owner = row % 2, col % 2, (col < 2).astype(jnp.int32)
        slabs, own = own_panel(features)
        pieces = [spread(slab, col, cols_n) for slab in slabs]

        other = swap(own, "cols", cols_n, 1)
        gram, give = panel_gram(jnp.stack([side, core]), own, other)
        gram = add(gram, swap(give, "rows", rows_n, 1))

        flags = jnp.stack([side, core, owner])
        sums, shares = [], []
        for half in range(halves):
            piece = held(pieces[half], gram)
            twin = swap(piece, "cols", cols_n, 1)
            share = [slabs[half], other[half], piece, twin]
            give, keep = panel_products(flags, features, *share, gram)
            shares += share
            steps = sum_steps(keep, swap(give, "rows", rows_n, 1), row, rows_n)
            next(steps)
            sums.append(steps)
            if half < halves - 1:
                gram = add(gram, swap(gram, "rows", rows_n, bits[0]), give)

        lead, trail = sums
        last = lead.send(give)
        last = lead.send(last)
        for bit in bits[1:]:
            last = gram = add(gram, swap(gram, "rows", rows_n, bit), last)
        last = trail.send(last)
        gram = join(gram, swap(gram, "rows", rows_n, 1), side, last)
        last = lead.send(gram)
        arrived = spread(gram, col, cols_n)
        last = trail.send(last)
        gram = jnp.where(col < 2, gram, held(arrived, last))
        state = first_stage(core, gram, swap(gram, "cols", cols_n, 1), last)
        for k in range(1, STAGES - 1):
            near = lead.send(state)
            last = trail.send(near)
            state = later_stage(k, state, last)
        for _ in range(2 * len(bits) - 4):
            near = lead.send(state)
            last = trail.send(near)
        inverse = later_stage(STAGES - 1, state, last)
        far = trail.send(inverse)

        mine = [near, far]
        received = [swap(total, "rows", rows_n, 1) for total in mine]
        basis, q_high, q_low = panel_bases(flags, shares, inverse)
        outs = finish(side, features, q_high, q_low, inverse, mine, ())
        factor, trailing = finish(1 - side, features, q_high, q_low, inverse, received, outs)
        basis = basis.reshape(rows, halves, 2, LANES).transpose(0, 2, 1, 3).reshape(rows, 2, width)
        return (factor.reshape(2 * width, panels, 1, width), basis, trailing.reshape(features.shape))

    return on_device


def solution(mesh):
    placed = (P("rows", None, "cols", None),)
    return jax.shard_map(
        program(mesh.shape["rows"], mesh.shape["cols"]),
        mesh=mesh,
        in_specs=placed,
        out_specs=(
            P(None, None, "cols", None),
            P("rows", None, None),
            P("rows", None, "cols", None),
        ),
        check_vma=False,
    )
```

```python
import functools

import jax
import jax.numpy as jnp
from jax import lax
from jax.experimental import pallas as pl
from jax.experimental.pallas import tpu as pltpu
from jax.sharding import PartitionSpec as P

HIGHEST = lax.Precision.HIGHEST
LANES = 128
SUB = 8
F32 = jnp.float32
BF16 = jnp.bfloat16


def params():
    return pltpu.CompilerParams(vmem_limit_bytes=48 * 1024 * 1024)


def vmem_spec():
    return pl.BlockSpec(memory_space=pltpu.VMEM)


def smem_spec():
    return pl.BlockSpec(memory_space=pltpu.SMEM)


def split(value):
    high = value.astype(BF16)
    return high, (value - high.astype(F32)).astype(BF16)


NN = (((1,), (0,)), ((), ()))
NT = (((1,), (1,)), ((), ()))


def dot3(left, right, dims=NN):
    def one(a, b):
        return lax.dot_general(a, b, dims, preferred_element_type=F32)

    return one(left[0], right[0]) + (one(left[0], right[1]) + one(left[1], right[0]))


def panel_kernel(x_ref, *refs):
    slabs, both, sems = refs[:-2], refs[-2], refs[-1]
    copies = [
        pltpu.make_async_copy(x_ref.at[:, 0, half], both.at[half], sems.at[half])
        for half in range(len(slabs))
    ]
    for copy in copies:
        copy.start()
    for half, slab in enumerate(slabs):
        copies[half].wait()
        slab[...] = both[half]


def own_panel(features):
    rows, panels, _, width = features.shape
    halves = width // LANES
    slab = jax.ShapeDtypeStruct((rows, LANES), F32)
    *slabs, both = pl.pallas_call(
        panel_kernel,
        in_specs=[pl.BlockSpec(memory_space=pltpu.HBM)],
        out_specs=[vmem_spec()] * (halves + 1),
        out_shape=[slab] * halves + [jax.ShapeDtypeStruct((halves, rows, LANES), F32)],
        scratch_shapes=[pltpu.SemaphoreType.DMA((halves,))],
        compiler_params=params(),
        cost_estimate=cost(2),
        name="own_panel",
    )(features.reshape(rows, panels, halves, LANES))
    return slabs, both


def any_spec():
    return pl.BlockSpec(memory_space=pl.ANY)


def cost(micros=0):
    return pl.CostEstimate(flops=1 + micros * 10 ** 9, bytes_accessed=1, transcendentals=0)


def held_kernel(value_ref, *refs):
    del value_ref, refs


def held(value, *after):
    return pl.pallas_call(
        held_kernel,
        in_specs=[any_spec()] * (1 + len(after)),
        out_specs=any_spec(),
        out_shape=jax.ShapeDtypeStruct(value.shape, value.dtype),
        input_output_aliases={0: 0},
        compiler_params=params(),
        cost_estimate=cost(),
        name="held",
    )(value, *after)


def halve_kernel(flag_ref, mine_ref, got_ref, *refs):
    keep_ref, give_ref = refs[-2:]
    half = keep_ref.shape[0]
    near = pl.multiple_of(flag_ref[0] * half, half)
    far = pl.multiple_of((1 - flag_ref[0]) * half, half)
    give_ref[...] = mine_ref[pl.ds(far, half), :] + got_ref[pl.ds(far, half), :]
    keep_ref[...] = mine_ref[pl.ds(near, half), :] + got_ref[pl.ds(near, half), :]


def halve(mine, got, flag, *after):
    rows, lanes = mine.shape
    half = jax.ShapeDtypeStruct((rows // 2, lanes), F32)
    return pl.pallas_call(
        halve_kernel,
        in_specs=[smem_spec()] + [vmem_spec()] * 2 + [any_spec()] * len(after),
        out_specs=[vmem_spec()] * 2,
        out_shape=[half, half],
        compiler_params=params(),
        cost_estimate=cost(),
        name="halve",
    )(flag.reshape(1), mine, got, *after)


def add_kernel(mine_ref, got_ref, *refs):
    refs[-1][...] = mine_ref[...] + got_ref[...]


def add(mine, got, *after):
    return pl.pallas_call(
        add_kernel,
        in_specs=[vmem_spec()] * 2 + [any_spec()] * len(after),
        out_specs=vmem_spec(),
        out_shape=jax.ShapeDtypeStruct(mine.shape, F32),
        compiler_params=params(),
        cost_estimate=cost(),
        name="add",
    )(mine, got, *after)


def join_kernel(flag_ref, mine_ref, got_ref, *refs):
    out_ref = refs[-1]
    half = mine_ref.shape[0]
    out_ref[pl.ds(pl.multiple_of(flag_ref[0] * half, half), half), :] = mine_ref[...]
    out_ref[pl.ds(pl.multiple_of((1 - flag_ref[0]) * half, half), half), :] = got_ref[...]


def join(mine, got, flag, *after):
    rows, lanes = mine.shape
    return pl.pallas_call(
        join_kernel,
        in_specs=[smem_spec()] + [vmem_spec()] * 2 + [any_spec()] * len(after),
        out_specs=vmem_spec(),
        out_shape=jax.ShapeDtypeStruct((2 * rows, lanes), F32),
        compiler_params=params(),
        cost_estimate=cost(),
        name="join",
    )(flag.reshape(1), mine, got, *after)


def gram_kernel(flags_ref, a_ref, b_ref, keep_ref, give_ref, work_ref):
    flag, core = flags_ref[0], flags_ref[1]

    def pick(zero, one):
        return jnp.where(core == 0, zero, one)

    own = jnp.concatenate([a_ref[0], a_ref[1]], axis=1)
    other = jnp.concatenate([b_ref[0], b_ref[1]], axis=1)
    first = pick(own, other)
    cross = pick(b_ref[0], a_ref[1])
    left = split(jnp.concatenate([own.T, cross.T], axis=0))
    width = own.shape[1]
    mine = dot3(tuple(part[:width] for part in left), split(own))
    mixed = dot3(tuple(part[width:] for part in left), split(first))
    parts = [mine[:LANES, :LANES], mine[LANES:, :LANES], mine[LANES:, LANES:],
             mixed[:, :LANES], mixed[:, LANES:]]
    for i, part in enumerate(parts):
        work_ref[i * LANES:(i + 1) * LANES, :] = part
    half = keep_ref.shape[0]
    keep_ref[...] = work_ref[pl.ds(pl.multiple_of(flag * half, half), half), :]
    give_ref[...] = work_ref[pl.ds(pl.multiple_of((1 - flag) * half, half), half), :]


def panel_gram(flags, own, other):
    half = jax.ShapeDtypeStruct((5 * LANES // 2, LANES), F32)
    return pl.pallas_call(
        gram_kernel,
        in_specs=[smem_spec(), vmem_spec(), vmem_spec()],
        out_specs=[vmem_spec()] * 2,
        out_shape=[half, half],
        scratch_shapes=[pltpu.VMEM((5 * LANES, LANES), F32)],
        compiler_params=params(),
        cost_estimate=cost(1),
        name="panel_gram",
    )(flags, own, other)


def fetch(x_ref, first, slabs_ref, sems):
    copies = []
    for i in range(slabs_ref.shape[0]):
        halves = x_ref.shape[2]
        source = x_ref.at[:, first + i // halves, i % halves]
        copies.append(pltpu.make_async_copy(source, slabs_ref.at[i], sems.at[i]))
    for copy in copies:
        copy.start()
    return copies


def times_columns(left, copies, slabs_ref, out_ref):
    for copy in copies:
        copy.wait()
    right = jnp.concatenate([slabs_ref[i] for i in range(slabs_ref.shape[0])], axis=1)
    value = dot3(left, split(right))
    height = value.shape[0]
    for i in range(slabs_ref.shape[0]):
        out_ref[i * height:(i + 1) * height, :] = value[:, i * LANES:(i + 1) * LANES]


def choose(flags_ref, own, other, got, twin):
    mine = jnp.where(flags_ref[2] == 1, own, got)
    paired = jnp.where(flags_ref[2] == 1, other, twin)
    zero = jnp.where(flags_ref[1] == 0, mine, paired)
    one = jnp.where(flags_ref[1] == 0, paired, mine)
    return zero, one


def product_kernel(flags_ref, x_ref, own_ref, other_ref, got_ref, twin_ref, *refs):
    give_ref, keep_ref, far_ref, near_ref, sems = refs[-5:]
    panels = x_ref.shape[1] // 2
    far = fetch(x_ref, (1 - flags_ref[0]) * panels, far_ref, sems.at[0])
    near = fetch(x_ref, flags_ref[0] * panels, near_ref, sems.at[1])
    zero, one = choose(flags_ref, own_ref[...], other_ref[...], got_ref[...], twin_ref[...])
    left = split(jnp.concatenate([zero, one], axis=1).T)
    times_columns(left, far, far_ref, give_ref)
    times_columns(left, near, near_ref, keep_ref)


def panel_products(flags, features, own, other, got, twin, *after):
    rows, panels, _, width = features.shape
    count = panels * width // LANES // 2
    x = features.reshape(rows, panels, width // LANES, LANES)
    out = jax.ShapeDtypeStruct((count * 2 * LANES, LANES), F32)
    return pl.pallas_call(
        product_kernel,
        in_specs=[smem_spec(), pl.BlockSpec(memory_space=pltpu.HBM)]
        + [vmem_spec()] * 4 + [any_spec()] * len(after),
        out_specs=[vmem_spec()] * 2,
        out_shape=[out, out],
        scratch_shapes=[pltpu.VMEM((count, rows, LANES), F32)] * 2
        + [pltpu.SemaphoreType.DMA((2, count))],
        compiler_params=params(),
        cost_estimate=cost(4),
        name="panel_products",
    )(flags, x, own, other, got, twin, *after)


def lane_copy(value, lane):
    return jnp.broadcast_to(value[:, lane:lane + 1], value.shape)


def row_copy(value, row):
    return jnp.broadcast_to(value[row:row + 1, :], value.shape)


def inverse_factor(block):
    groups = LANES // SUB
    lane = lax.broadcasted_iota(jnp.int32, (SUB, LANES), 1)
    sub = lax.broadcasted_iota(jnp.int32, (SUB, LANES), 0)
    work = [block[SUB * g:SUB * (g + 1), :] for g in range(groups)]
    result = []
    for g in range(groups):
        start = SUB * g
        panel = work[g]
        inside = (lane >= start) & (lane < start + SUB)
        cols = [lane_copy(panel, start + j) for j in range(SUB)]
        c = {(s, j): row_copy(cols[j], s) for j in range(SUB) for s in range(j, SUB)}
        mult, recip, diag = {}, [], []
        for i in range(0, SUB, 2):
            a, b, d = c[i, i], c[i + 1, i], c[i + 1, i + 1]
            det = a * d - b * b
            ra, rdet = 1.0 / a, 1.0 / det
            f = b * ra
            mult[i + 1, i] = f
            rb = a * rdet
            recip += [ra, rb]
            diag += [a, det * ra]
            for s in range(i + 2, SUB):
                mult[s, i] = c[s, i] * ra
                c[s, i + 1] = c[s, i + 1] - f * c[s, i]
                mult[s, i + 1] = c[s, i + 1] * rb
            for s in range(i + 2, SUB):
                for t in range(i + 2, s + 1):
                    c[s, t] = (c[s, t] - mult[s, i] * c[t, i]) - mult[s, i + 1] * c[t, i + 1]
        unit = jnp.where(inside, jnp.where(lane == start + sub, 1.0, 0.0), panel)
        upper = []
        for s in range(SUB):
            row = row_copy(unit, s)
            for i in range(s):
                row = row - mult[s, i] * upper[i]
            upper.append(row)
        scaled = [upper[s] * recip[s] for s in range(SUB)]
        nxt = g + 1
        if nxt < groups:
            old = work[nxt]
            new = jnp.where(inside, 0.0, old)
            v = []
            for j in range(SUB):
                e = lane_copy(old, start + j)
                for i in range(j):
                    e = e - mult[j, i] * v[i]
                v.append(e)
                new = new - e * scaled[j]
            work[nxt] = new
            nxt += 1
        if nxt < groups:
            solved = [None] * SUB
            for s in reversed(range(SUB)):
                row = scaled[s]
                for t in reversed(range(s + 1, SUB)):
                    row = row - mult[t, s] * solved[t]
                solved[s] = row
        for later in range(nxt, groups):
            old = work[later]
            new = jnp.where(inside, 0.0, old)
            for j in range(SUB):
                new = new - lane_copy(old, start + j) * solved[j]
            work[later] = new
        rows, dg = upper[0], diag[0]
        for s in range(1, SUB):
            rows = jnp.where(sub == s, upper[s], rows)
            dg = jnp.where(sub == s, diag[s], dg)
        result.append(jnp.where(lane < start + SUB, rows * lax.rsqrt(dg), 0.0))
    return jnp.concatenate(result, axis=0)


def dot6(a, b, dims=NN):
    return lax.dot_general(a, b, dims, precision=HIGHEST, preferred_element_type=F32)


STAGES = 4


def place(i, j):
    return i * (i + 1) // 2 + j


def stage(k, s):
    m = inverse_factor(s[k, k])
    for j in range(k):
        s[k, j] = dot6(m, s[k, j])
    low = {i: dot6(s[i, k], m, NT) for i in range(k + 1, STAGES)}
    s[k, k] = m
    for i in range(k + 1, STAGES):
        for j in range(k + 1, i + 1):
            s[i, j] = s[i, j] - dot6(low[i], low[j], NT)
        for j in range(k):
            s[i, j] = s[i, j] - dot6(low[i], s[k, j])
        s[i, k] = -dot6(low[i], m)


def first_stage_kernel(core_ref, mine_ref, twin_ref, *refs):
    out_ref = refs[-1]
    zero = jnp.where(core_ref[0] == 0, mine_ref[...], twin_ref[...])
    one = jnp.where(core_ref[0] == 0, twin_ref[...], mine_ref[...])

    def block(value, i):
        return value[i * LANES:(i + 1) * LANES]

    s = {
        (0, 0): block(zero, 0), (1, 0): block(zero, 1), (1, 1): block(zero, 2),
        (2, 0): block(zero, 3), (2, 1): block(zero, 4),
        (2, 2): block(one, 0), (3, 2): block(one, 1), (3, 3): block(one, 2),
        (3, 0): block(one, 3), (3, 1): block(one, 4),
    }
    stage(0, s)
    for (i, j), value in s.items():
        out_ref[place(i, j)] = value


def later_stage_kernel(k, in_ref, *refs):
    s = {(i, j): in_ref[place(i, j)] for i in range(STAGES) for j in range(i + 1)}
    stage(k, s)
    for (i, j), value in s.items():
        refs[-1][place(i, j)] = value


def stage_call(kernel, name, operands, scalars, after):
    return pl.pallas_call(
        kernel,
        in_specs=[smem_spec()] * scalars + [vmem_spec()] * (len(operands) - scalars)
        + [any_spec()] * len(after),
        out_specs=vmem_spec(),
        out_shape=jax.ShapeDtypeStruct((place(STAGES, 0), LANES, LANES), F32),
        compiler_params=params(),
        cost_estimate=cost(),
        name=name,
    )(*operands, *after)


def first_stage(core, mine, twin, *after):
    return stage_call(first_stage_kernel, "factor_0", [core.reshape(1), mine, twin], 1, after)


def later_stage(k, state, *after):
    return stage_call(functools.partial(later_stage_kernel, k), "factor_%d" % k, [state], 0, after)


def packed(ref):
    zero = jnp.zeros((LANES, LANES), F32)
    rows = [
        jnp.concatenate([ref[place(i, j)] if j <= i else zero for j in range(STAGES)], axis=1)
        for i in range(STAGES)
    ]
    return jnp.concatenate(rows, axis=0)


def basis_kernel(flags_ref, *refs):
    halves = (len(refs) - 5) // 4
    x_ref, lines_ref, high_ref, low_ref = refs[4 * halves], *refs[-3:]
    zeros, ones = [], []
    for half in range(halves):
        zero, one = choose(flags_ref, *(ref[...] for ref in refs[4 * half:4 * half + 4]))
        zeros.append(zero)
        ones.append(one)
    rows = zeros[0].shape[0]
    panels = jnp.concatenate(zeros + ones, axis=1)
    q = dot3(split(panels), split(packed(x_ref)), NT)
    high, low = split(q)
    high_ref[...] = high
    low_ref[...] = low
    for panel in range(2):
        for half in range(2):
            k = 2 * panel + half
            lines_ref[pl.ds(2 * half + panel, rows, stride=4), :] = q[:, k * LANES:(k + 1) * LANES]


def panel_bases(flags, slabs, inverse, after):
    rows = slabs[0].shape[0]
    size = STAGES * LANES
    step = 256
    piece = pl.BlockSpec((step, LANES), lambda i: (i, 0))
    wide = pl.BlockSpec((step, size), lambda i: (i, 0))
    return pl.pallas_call(
        basis_kernel,
        grid=(rows // step,),
        in_specs=[smem_spec()] + [piece] * len(slabs) + [vmem_spec(), any_spec()],
        out_specs=[pl.BlockSpec((4 * step, LANES), lambda i: (i, 0)), wide, wide],
        out_shape=[
            jax.ShapeDtypeStruct((4 * rows, LANES), F32),
            jax.ShapeDtypeStruct((rows, size), BF16),
            jax.ShapeDtypeStruct((rows, size), BF16),
        ],
        compiler_params=params(),
        cost_estimate=cost(),
        name="panel_bases",
    )(flags, *slabs, inverse, after)


def trailing_kernel(flags_ref, x_ref, qh_ref, ql_ref, inv_ref, h0_ref, h1_ref, *refs):
    factor_ref, out_ref, q_ref, x_slabs, w_slabs, out_slabs, q_sems, x_sems, w_sems, out_sems = refs[-10:]
    count, rows = x_slabs.shape[0], x_slabs.shape[1]
    halves = x_ref.shape[2]
    first = flags_ref[0] * x_ref.shape[1] // 2
    fetched = [
        pltpu.make_async_copy(ref, q_ref.at[i], q_sems.at[i]) for i, ref in enumerate((qh_ref, ql_ref))
    ]
    for copy in fetched:
        copy.start()
    fetched += fetch(x_ref, first, x_slabs, x_sems)
    columns = []
    for i in range(count):
        at = [(2 * i + p) * LANES for p in range(2)]
        columns.append(jnp.concatenate([ref[a:a + LANES] for a in at for ref in (h0_ref, h1_ref)], axis=0))
    w = dot3(split(packed(inv_ref)), split(jnp.concatenate(columns, axis=1)))
    sent = []
    for i in range(count):
        w_slabs[i] = w[:, i * LANES:(i + 1) * LANES]
        target = factor_ref.at[:, first + i // halves, i % halves]
        sent.append(pltpu.make_async_copy(w_slabs.at[i], target, w_sems.at[i]))
        sent[-1].start()
    right = split(w)
    for copy in fetched:
        copy.wait()
    chunks = out_sems.shape[0]
    step = rows // chunks
    for chunk in range(chunks):
        here = pl.ds(chunk * step, step)
        term = dot3((q_ref[0, here, :], q_ref[1, here, :]), right)
        for i in range(count):
            out_slabs[i, here, :] = x_slabs[i, here, :] - term[:, i * LANES:(i + 1) * LANES]
            target = out_ref.at[here, first + i // halves, i % halves]
            sent.append(pltpu.make_async_copy(out_slabs.at[i, here], target, out_sems.at[chunk, i]))
            sent[-1].start()
    for copy in sent:
        copy.wait()


def finish(side, features, q_high, q_low, inverse, pieces, outs, *after):
    rows, panels, _, width = features.shape
    halves = width // LANES
    size = q_high.shape[1]
    count = panels * halves // 2
    x = features.reshape(rows, panels, halves, LANES)
    hbm = pl.BlockSpec(memory_space=pltpu.HBM)
    chunks = 4
    extra = len(outs)
    return pl.pallas_call(
        trailing_kernel,
        in_specs=[smem_spec(), hbm] + [any_spec()] * 2 + [vmem_spec()] * 3 + [hbm] * extra + [any_spec()] * len(after),
        out_specs=[hbm, hbm],
        out_shape=[
            jax.ShapeDtypeStruct((size, panels, halves, LANES), F32),
            jax.ShapeDtypeStruct(x.shape, F32),
        ],
        scratch_shapes=[
            pltpu.VMEM((2, rows, size), BF16),
            pltpu.VMEM((count, rows, LANES), F32),
            pltpu.VMEM((count, size, LANES), F32),
            pltpu.VMEM((count, rows, LANES), F32),
            pltpu.SemaphoreType.DMA((2,)),
            pltpu.SemaphoreType.DMA((count,)),
            pltpu.SemaphoreType.DMA((count,)),
            pltpu.SemaphoreType.DMA((chunks, count)),
        ],
        input_output_aliases={7 + i: i for i in range(extra)},
        compiler_params=params(),
        cost_estimate=cost(5),
        name="finish",
    )(side.reshape(1), x, q_high, q_low, inverse, *pieces, *outs, *after)


def swap(value, axis, size, bit):
    return lax.ppermute(value, axis, [(i, i ^ bit) for i in range(size)])


def spread(value, col, cols):
    got, span = None, 2
    while span < cols:
        new = lax.ppermute(value, "cols", [(i, i + span) for i in range(min(span, cols - span))])
        got = new if got is None else jnp.where(col < span, got, new)
        span *= 2
        if span < cols:
            value = jnp.where(col < 2, value, got)
    return got


def bits_of(size):
    bits, bit = [], 1
    while bit < size:
        bits.append(bit)
        bit *= 2
    return bits


def sum_steps(mine, got, row, rows):
    bits = bits_of(rows)[1:]
    after = yield
    for bit in bits:
        mine, give = halve(mine, got, (row // bit) % 2, after)
        got = swap(give, "rows", rows, bit)
        after = yield mine
    value = add(mine, got, after)
    for bit in reversed(bits):
        got = swap(value, "rows", rows, bit)
        after = yield value
        value = join(value, got, (row // bit) % 2, after)
    yield value


def program(rows_n, cols_n):
    bits = bits_of(rows_n)[1:]

    def on_device(features):
        rows, panels, _, width = features.shape
        halves = width // LANES
        row, col = lax.axis_index("rows"), lax.axis_index("cols")
        side, core, owner = row % 2, col % 2, (col < 2).astype(jnp.int32)
        slabs, own = own_panel(features)
        pieces = [spread(slab, col, cols_n) for slab in slabs]

        other = swap(own, "cols", cols_n, 1)
        gram, give = panel_gram(jnp.stack([side, core]), own, other)
        gram = add(gram, swap(give, "rows", rows_n, 1))
        order = gram = add(gram, swap(gram, "rows", rows_n, bits[0]))
        for bit in bits[1:]:
            gram = add(gram, swap(gram, "rows", rows_n, bit))

        flags = jnp.stack([side, core, owner])
        sums, shares = [], []
        for half in range(halves):
            piece = held(pieces[half], order)
            twin = swap(piece, "cols", cols_n, 1)
            share = [slabs[half], other[half], piece, twin]
            give, keep = panel_products(flags, features, *share, gram)
            if half == 0:
                gram = join(gram, swap(gram, "rows", rows_n, 1), side)
            order = give
            shares += share
            steps = sum_steps(keep, swap(give, "rows", rows_n, 1), row, rows_n)
            next(steps)
            sums.append(steps)

        lead, trail = sums
        arrived, last = spread(gram, col, cols_n), give
        steps = 2 * len(bits) + 1
        for k in range(steps):
            last = near = lead.send(last)
            if k == 0:
                gram = jnp.where(col < 2, gram, held(arrived, last))
                last = state = first_stage(core, gram, swap(gram, "cols", cols_n, 1), last)
            elif k < STAGES:
                last = state = later_stage(k, state, last)
            if k == steps - 1:
                basis, q_high, q_low = panel_bases(flags, shares, state, near)
                last = q_high
            last = far = trail.send(last)

        mine = [near, far]
        received = [swap(total, "rows", rows_n, 1) for total in mine]
        inverse = state
        outs = finish(side, features, q_high, q_low, inverse, mine, ())
        factor, trailing = finish(1 - side, features, q_high, q_low, inverse, received, outs)
        basis = basis.reshape(rows, halves, 2, LANES).transpose(0, 2, 1, 3).reshape(rows, 2, width)
        return (factor.reshape(2 * width, panels, 1, width), basis, trailing.reshape(features.shape))

    return on_device


def solution(mesh):
    placed = (P("rows", None, "cols", None),)
    return jax.shard_map(
        program(mesh.shape["rows"], mesh.shape["cols"]),
        mesh=mesh,
        in_specs=placed,
        out_specs=(
            P(None, None, "cols", None),
            P("rows", None, None),
            P("rows", None, "cols", None),
        ),
        check_vma=False,
    )
```

```python
import functools

import jax
import jax.numpy as jnp
from jax import lax
from jax.experimental import pallas as pl
from jax.experimental.pallas import tpu as pltpu
from jax.sharding import PartitionSpec as P

HIGHEST = lax.Precision.HIGHEST
LANES = 128
SUB = 8
F32 = jnp.float32
BF16 = jnp.bfloat16


def params():
    return pltpu.CompilerParams(vmem_limit_bytes=48 * 1024 * 1024)


def vmem_spec():
    return pl.BlockSpec(memory_space=pltpu.VMEM)


def smem_spec():
    return pl.BlockSpec(memory_space=pltpu.SMEM)


def split(value):
    high = value.astype(BF16)
    return high, (value - high.astype(F32)).astype(BF16)


NN = (((1,), (0,)), ((), ()))
NT = (((1,), (1,)), ((), ()))


def dot3(left, right, dims=NN):
    def one(a, b):
        return lax.dot_general(a, b, dims, preferred_element_type=F32)

    return one(left[0], right[0]) + (one(left[0], right[1]) + one(left[1], right[0]))


def panel_kernel(x_ref, *refs):
    slabs, both, sems = refs[:-2], refs[-2], refs[-1]
    copies = [
        pltpu.make_async_copy(x_ref.at[:, 0, half], both.at[half], sems.at[half])
        for half in range(len(slabs))
    ]
    for copy in copies:
        copy.start()
    for half, slab in enumerate(slabs):
        copies[half].wait()
        slab[...] = both[half]


def own_panel(features):
    rows, panels, _, width = features.shape
    halves = width // LANES
    slab = jax.ShapeDtypeStruct((rows, LANES), F32)
    *slabs, both = pl.pallas_call(
        panel_kernel,
        in_specs=[pl.BlockSpec(memory_space=pltpu.HBM)],
        out_specs=[vmem_spec()] * (halves + 1),
        out_shape=[slab] * halves + [jax.ShapeDtypeStruct((halves, rows, LANES), F32)],
        scratch_shapes=[pltpu.SemaphoreType.DMA((halves,))],
        compiler_params=params(),
        cost_estimate=cost(2),
        name="own_panel",
    )(features.reshape(rows, panels, halves, LANES))
    return slabs, both


def any_spec():
    return pl.BlockSpec(memory_space=pl.ANY)


def cost(micros=0):
    return pl.CostEstimate(flops=1 + micros * 10 ** 9, bytes_accessed=1, transcendentals=0)


def held_kernel(value_ref, *refs):
    del value_ref, refs


def held(value, *after):
    return pl.pallas_call(
        held_kernel,
        in_specs=[any_spec()] * (1 + len(after)),
        out_specs=any_spec(),
        out_shape=jax.ShapeDtypeStruct(value.shape, value.dtype),
        input_output_aliases={0: 0},
        compiler_params=params(),
        cost_estimate=cost(),
        name="held",
    )(value, *after)


def halve_kernel(flag_ref, mine_ref, got_ref, *refs):
    keep_ref, give_ref = refs[-2:]
    half = keep_ref.shape[0]
    near = pl.multiple_of(flag_ref[0] * half, half)
    far = pl.multiple_of((1 - flag_ref[0]) * half, half)
    give_ref[...] = mine_ref[pl.ds(far, half), :] + got_ref[pl.ds(far, half), :]
    keep_ref[...] = mine_ref[pl.ds(near, half), :] + got_ref[pl.ds(near, half), :]


def halve(mine, got, flag, *after):
    rows, lanes = mine.shape
    half = jax.ShapeDtypeStruct((rows // 2, lanes), F32)
    return pl.pallas_call(
        halve_kernel,
        in_specs=[smem_spec()] + [vmem_spec()] * 2 + [any_spec()] * len(after),
        out_specs=[vmem_spec()] * 2,
        out_shape=[half, half],
        compiler_params=params(),
        cost_estimate=cost(),
        name="halve",
    )(flag.reshape(1), mine, got, *after)


def add_kernel(mine_ref, got_ref, *refs):
    refs[-1][...] = mine_ref[...] + got_ref[...]


def add(mine, got, *after):
    return pl.pallas_call(
        add_kernel,
        in_specs=[vmem_spec()] * 2 + [any_spec()] * len(after),
        out_specs=vmem_spec(),
        out_shape=jax.ShapeDtypeStruct(mine.shape, F32),
        compiler_params=params(),
        cost_estimate=cost(),
        name="add",
    )(mine, got, *after)


def join_kernel(flag_ref, mine_ref, got_ref, *refs):
    out_ref = refs[-1]
    half = mine_ref.shape[0]
    out_ref[pl.ds(pl.multiple_of(flag_ref[0] * half, half), half), :] = mine_ref[...]
    out_ref[pl.ds(pl.multiple_of((1 - flag_ref[0]) * half, half), half), :] = got_ref[...]


def join(mine, got, flag, *after):
    rows, lanes = mine.shape
    return pl.pallas_call(
        join_kernel,
        in_specs=[smem_spec()] + [vmem_spec()] * 2 + [any_spec()] * len(after),
        out_specs=vmem_spec(),
        out_shape=jax.ShapeDtypeStruct((2 * rows, lanes), F32),
        compiler_params=params(),
        cost_estimate=cost(),
        name="join",
    )(flag.reshape(1), mine, got, *after)


def gram_kernel(flags_ref, a_ref, b_ref, keep_ref, give_ref, work_ref):
    flag, core = flags_ref[0], flags_ref[1]

    def pick(zero, one):
        return jnp.where(core == 0, zero, one)

    own = jnp.concatenate([a_ref[0], a_ref[1]], axis=1)
    other = jnp.concatenate([b_ref[0], b_ref[1]], axis=1)
    first = pick(own, other)
    cross = pick(b_ref[0], a_ref[1])
    left = split(jnp.concatenate([own.T, cross.T], axis=0))
    width = own.shape[1]
    mine = dot3(tuple(part[:width] for part in left), split(own))
    mixed = dot3(tuple(part[width:] for part in left), split(first))
    parts = [mine[:LANES, :LANES], mine[LANES:, :LANES], mine[LANES:, LANES:],
             mixed[:, :LANES], mixed[:, LANES:]]
    for i, part in enumerate(parts):
        work_ref[i * LANES:(i + 1) * LANES, :] = part
    half = keep_ref.shape[0]
    keep_ref[...] = work_ref[pl.ds(pl.multiple_of(flag * half, half), half), :]
    give_ref[...] = work_ref[pl.ds(pl.multiple_of((1 - flag) * half, half), half), :]


def panel_gram(flags, own, other):
    half = jax.ShapeDtypeStruct((5 * LANES // 2, LANES), F32)
    return pl.pallas_call(
        gram_kernel,
        in_specs=[smem_spec(), vmem_spec(), vmem_spec()],
        out_specs=[vmem_spec()] * 2,
        out_shape=[half, half],
        scratch_shapes=[pltpu.VMEM((5 * LANES, LANES), F32)],
        compiler_params=params(),
        cost_estimate=cost(1),
        name="panel_gram",
    )(flags, own, other)


def fetch(x_ref, first, slabs_ref, sems):
    copies = []
    for i in range(slabs_ref.shape[0]):
        halves = x_ref.shape[2]
        source = x_ref.at[:, first + i // halves, i % halves]
        copies.append(pltpu.make_async_copy(source, slabs_ref.at[i], sems.at[i]))
    for copy in copies:
        copy.start()
    return copies


def times_columns(left, copies, slabs_ref, out_ref):
    for copy in copies:
        copy.wait()
    right = jnp.concatenate([slabs_ref[i] for i in range(slabs_ref.shape[0])], axis=1)
    value = dot3(left, split(right))
    height = value.shape[0]
    for i in range(slabs_ref.shape[0]):
        out_ref[i * height:(i + 1) * height, :] = value[:, i * LANES:(i + 1) * LANES]


def choose(flags_ref, own, other, got, twin):
    mine = jnp.where(flags_ref[2] == 1, own, got)
    paired = jnp.where(flags_ref[2] == 1, other, twin)
    zero = jnp.where(flags_ref[1] == 0, mine, paired)
    one = jnp.where(flags_ref[1] == 0, paired, mine)
    return zero, one


def product_kernel(half, flags_ref, x_ref, own_ref, other_ref, got_ref, twin_ref, *refs):
    give_ref, keep_ref, pair_ref, far_ref, near_ref, pair_sems, sems = refs[-7:]

    def load(*sources):
        for i, source in enumerate(sources):
            pltpu.make_async_copy(source, pair_ref.at[i], pair_sems.at[i]).start()

    @pl.when(flags_ref[2] == 1)
    def _():
        load(own_ref, other_ref.at[half])

    @pl.when(flags_ref[2] != 1)
    def _():
        load(got_ref, twin_ref)

    panels = x_ref.shape[1] // 2
    far = fetch(x_ref, (1 - flags_ref[0]) * panels, far_ref, sems.at[0])
    near = fetch(x_ref, flags_ref[0] * panels, near_ref, sems.at[1])
    for i in range(2):
        pltpu.make_async_copy(own_ref, pair_ref.at[i], pair_sems.at[i]).wait()
    zero, one = pair_ref[flags_ref[1]], pair_ref[1 - flags_ref[1]]
    left = split(jnp.concatenate([zero, one], axis=1).T)
    times_columns(left, far, far_ref, give_ref)
    times_columns(left, near, near_ref, keep_ref)


def panel_products(half, flags, features, own, other, got, twin, *after):
    rows, panels, _, width = features.shape
    count = panels * width // LANES // 2
    x = features.reshape(rows, panels, width // LANES, LANES)
    out = jax.ShapeDtypeStruct((count * 2 * LANES, LANES), F32)
    return pl.pallas_call(
        functools.partial(product_kernel, half),
        in_specs=[smem_spec(), pl.BlockSpec(memory_space=pltpu.HBM)]
        + [any_spec()] * (4 + len(after)),
        out_specs=[vmem_spec()] * 2,
        out_shape=[out, out],
        scratch_shapes=[pltpu.VMEM((2, rows, LANES), F32)]
        + [pltpu.VMEM((count, rows, LANES), F32)] * 2
        + [pltpu.SemaphoreType.DMA((2,)), pltpu.SemaphoreType.DMA((2, count))],
        compiler_params=params(),
        cost_estimate=cost(4),
        name="panel_products",
    )(flags, x, own, other, got, twin, *after)


def lane_copy(value, lane):
    return jnp.broadcast_to(value[:, lane:lane + 1], value.shape)


def row_copy(value, row):
    return jnp.broadcast_to(value[row:row + 1, :], value.shape)


def inverse_factor(block):
    groups = LANES // SUB
    lane = lax.broadcasted_iota(jnp.int32, (SUB, LANES), 1)
    sub = lax.broadcasted_iota(jnp.int32, (SUB, LANES), 0)
    work = [block[SUB * g:SUB * (g + 1), :] for g in range(groups)]
    result = []
    for g in range(groups):
        start = SUB * g
        panel = work[g]
        inside = (lane >= start) & (lane < start + SUB)
        cols = [lane_copy(panel, start + j) for j in range(SUB)]
        c = {(s, j): row_copy(cols[j], s) for j in range(SUB) for s in range(j, SUB)}
        mult, recip, diag = {}, [], []
        for i in range(0, SUB, 2):
            a, b, d = c[i, i], c[i + 1, i], c[i + 1, i + 1]
            det = a * d - b * b
            ra, rdet = 1.0 / a, 1.0 / det
            f = b * ra
            mult[i + 1, i] = f
            rb = a * rdet
            recip += [ra, rb]
            diag += [a, det * ra]
            for s in range(i + 2, SUB):
                mult[s, i] = c[s, i] * ra
                c[s, i + 1] = c[s, i + 1] - f * c[s, i]
                mult[s, i + 1] = c[s, i + 1] * rb
            for s in range(i + 2, SUB):
                for t in range(i + 2, s + 1):
                    c[s, t] = (c[s, t] - mult[s, i] * c[t, i]) - mult[s, i + 1] * c[t, i + 1]
        unit = jnp.where(inside, jnp.where(lane == start + sub, 1.0, 0.0), panel)
        upper = []
        for s in range(SUB):
            row = row_copy(unit, s)
            for i in range(s):
                row = row - mult[s, i] * upper[i]
            upper.append(row)
        scaled = [upper[s] * recip[s] for s in range(SUB)]
        nxt = g + 1
        if nxt < groups:
            old = work[nxt]
            new = jnp.where(inside, 0.0, old)
            v = []
            for j in range(SUB):
                e = lane_copy(old, start + j)
                for i in range(j):
                    e = e - mult[j, i] * v[i]
                v.append(e)
                new = new - e * scaled[j]
            work[nxt] = new
            nxt += 1
        if nxt < groups:
            solved = [None] * SUB
            for s in reversed(range(SUB)):
                row = scaled[s]
                for t in reversed(range(s + 1, SUB)):
                    row = row - mult[t, s] * solved[t]
                solved[s] = row
        for later in range(nxt, groups):
            old = work[later]
            new = jnp.where(inside, 0.0, old)
            for j in range(SUB):
                new = new - lane_copy(old, start + j) * solved[j]
            work[later] = new
        rows, dg = upper[0], diag[0]
        for s in range(1, SUB):
            rows = jnp.where(sub == s, upper[s], rows)
            dg = jnp.where(sub == s, diag[s], dg)
        result.append(jnp.where(lane < start + SUB, rows * lax.rsqrt(dg), 0.0))
    return jnp.concatenate(result, axis=0)


def dot6(a, b, dims=NN):
    return lax.dot_general(a, b, dims, precision=HIGHEST, preferred_element_type=F32)


STAGES = 4


def place(i, j):
    return i * (i + 1) // 2 + j


def stage(k, s):
    m = inverse_factor(s[k, k])
    for j in range(k):
        s[k, j] = dot6(m, s[k, j])
    low = {i: dot6(s[i, k], m, NT) for i in range(k + 1, STAGES)}
    s[k, k] = m
    for i in range(k + 1, STAGES):
        for j in range(k + 1, i + 1):
            s[i, j] = s[i, j] - dot6(low[i], low[j], NT)
        for j in range(k):
            s[i, j] = s[i, j] - dot6(low[i], s[k, j])
        s[i, k] = -dot6(low[i], m)


def first_stage_kernel(core_ref, mine_ref, twin_ref, *refs):
    out_ref = refs[-1]
    zero = jnp.where(core_ref[0] == 0, mine_ref[...], twin_ref[...])
    one = jnp.where(core_ref[0] == 0, twin_ref[...], mine_ref[...])

    def block(value, i):
        return value[i * LANES:(i + 1) * LANES]

    s = {
        (0, 0): block(zero, 0), (1, 0): block(zero, 1), (1, 1): block(zero, 2),
        (2, 0): block(zero, 3), (2, 1): block(zero, 4),
        (2, 2): block(one, 0), (3, 2): block(one, 1), (3, 3): block(one, 2),
        (3, 0): block(one, 3), (3, 1): block(one, 4),
    }
    stage(0, s)
    for (i, j), value in s.items():
        out_ref[place(i, j)] = value


def later_stage_kernel(k, in_ref, *refs):
    s = {(i, j): in_ref[place(i, j)] for i in range(STAGES) for j in range(i + 1)}
    stage(k, s)
    for (i, j), value in s.items():
        refs[-1][place(i, j)] = value


def stage_call(kernel, name, operands, scalars, after):
    return pl.pallas_call(
        kernel,
        in_specs=[smem_spec()] * scalars + [vmem_spec()] * (len(operands) - scalars)
        + [any_spec()] * len(after),
        out_specs=vmem_spec(),
        out_shape=jax.ShapeDtypeStruct((place(STAGES, 0), LANES, LANES), F32),
        compiler_params=params(),
        cost_estimate=cost(),
        name=name,
    )(*operands, *after)


def first_stage(core, mine, twin, *after):
    return stage_call(first_stage_kernel, "factor_0", [core.reshape(1), mine, twin], 1, after)


def later_stage(k, state, *after):
    return stage_call(functools.partial(later_stage_kernel, k), "factor_%d" % k, [state], 0, after)


def packed(ref):
    zero = jnp.zeros((LANES, LANES), F32)
    rows = [
        jnp.concatenate([ref[place(i, j)] if j <= i else zero for j in range(STAGES)], axis=1)
        for i in range(STAGES)
    ]
    return jnp.concatenate(rows, axis=0)


def basis_kernel(flags_ref, *refs):
    halves = (len(refs) - 5) // 4
    x_ref, lines_ref, high_ref, low_ref = refs[4 * halves], *refs[-3:]
    zeros, ones = [], []
    for half in range(halves):
        zero, one = choose(flags_ref, *(ref[...] for ref in refs[4 * half:4 * half + 4]))
        zeros.append(zero)
        ones.append(one)
    rows = zeros[0].shape[0]
    panels = jnp.concatenate(zeros + ones, axis=1)
    q = dot3(split(panels), split(packed(x_ref)), NT)
    high, low = split(q)
    high_ref[...] = high
    low_ref[...] = low
    for panel in range(2):
        for half in range(2):
            k = 2 * panel + half
            lines_ref[pl.ds(2 * half + panel, rows, stride=4), :] = q[:, k * LANES:(k + 1) * LANES]


def panel_bases(flags, slabs, inverse, after):
    rows = slabs[0].shape[0]
    size = STAGES * LANES
    step = 256
    piece = pl.BlockSpec((step, LANES), lambda i: (i, 0))
    wide = pl.BlockSpec((step, size), lambda i: (i, 0))
    return pl.pallas_call(
        basis_kernel,
        grid=(rows // step,),
        in_specs=[smem_spec()] + [piece] * len(slabs) + [vmem_spec(), any_spec()],
        out_specs=[pl.BlockSpec((4 * step, LANES), lambda i: (i, 0)), wide, wide],
        out_shape=[
            jax.ShapeDtypeStruct((4 * rows, LANES), F32),
            jax.ShapeDtypeStruct((rows, size), BF16),
            jax.ShapeDtypeStruct((rows, size), BF16),
        ],
        compiler_params=params(),
        cost_estimate=cost(),
        name="panel_bases",
    )(flags, *slabs, inverse, after)


def trailing_kernel(flags_ref, x_ref, qh_ref, ql_ref, inv_ref, h0_ref, h1_ref, *refs):
    factor_ref, out_ref, q_ref, x_slabs, w_slabs, out_slabs, q_sems, x_sems, w_sems, out_sems = refs[-10:]
    count, rows = x_slabs.shape[0], x_slabs.shape[1]
    halves = x_ref.shape[2]
    first = flags_ref[0] * x_ref.shape[1] // 2
    fetched = [
        pltpu.make_async_copy(ref, q_ref.at[i], q_sems.at[i]) for i, ref in enumerate((qh_ref, ql_ref))
    ]
    for copy in fetched:
        copy.start()
    fetched += fetch(x_ref, first, x_slabs, x_sems)
    columns = []
    for i in range(count):
        at = [(2 * i + p) * LANES for p in range(2)]
        columns.append(jnp.concatenate([ref[a:a + LANES] for a in at for ref in (h0_ref, h1_ref)], axis=0))
    w = dot3(split(packed(inv_ref)), split(jnp.concatenate(columns, axis=1)))
    sent = []
    for i in range(count):
        w_slabs[i] = w[:, i * LANES:(i + 1) * LANES]
        target = factor_ref.at[:, first + i // halves, i % halves]
        sent.append(pltpu.make_async_copy(w_slabs.at[i], target, w_sems.at[i]))
        sent[-1].start()
    right = split(w)
    for copy in fetched:
        copy.wait()
    chunks = out_sems.shape[0]
    step = rows // chunks
    for chunk in range(chunks):
        here = pl.ds(chunk * step, step)
        term = dot3((q_ref[0, here, :], q_ref[1, here, :]), right)
        for i in range(count):
            out_slabs[i, here, :] = x_slabs[i, here, :] - term[:, i * LANES:(i + 1) * LANES]
            target = out_ref.at[here, first + i // halves, i % halves]
            sent.append(pltpu.make_async_copy(out_slabs.at[i, here], target, out_sems.at[chunk, i]))
            sent[-1].start()
    for copy in sent:
        copy.wait()


def finish(side, features, q_high, q_low, inverse, pieces, outs, *after):
    rows, panels, _, width = features.shape
    halves = width // LANES
    size = q_high.shape[1]
    count = panels * halves // 2
    x = features.reshape(rows, panels, halves, LANES)
    hbm = pl.BlockSpec(memory_space=pltpu.HBM)
    chunks = 4
    extra = len(outs)
    return pl.pallas_call(
        trailing_kernel,
        in_specs=[smem_spec(), hbm] + [any_spec()] * 2 + [vmem_spec()] * 3 + [hbm] * extra + [any_spec()] * len(after),
        out_specs=[hbm, hbm],
        out_shape=[
            jax.ShapeDtypeStruct((size, panels, halves, LANES), F32),
            jax.ShapeDtypeStruct(x.shape, F32),
        ],
        scratch_shapes=[
            pltpu.VMEM((2, rows, size), BF16),
            pltpu.VMEM((count, rows, LANES), F32),
            pltpu.VMEM((count, size, LANES), F32),
            pltpu.VMEM((count, rows, LANES), F32),
            pltpu.SemaphoreType.DMA((2,)),
            pltpu.SemaphoreType.DMA((count,)),
            pltpu.SemaphoreType.DMA((count,)),
            pltpu.SemaphoreType.DMA((chunks, count)),
        ],
        input_output_aliases={7 + i: i for i in range(extra)},
        compiler_params=params(),
        cost_estimate=cost(5),
        name="finish",
    )(side.reshape(1), x, q_high, q_low, inverse, *pieces, *outs, *after)


def swap(value, axis, size, bit):
    return lax.ppermute(value, axis, [(i, i ^ bit) for i in range(size)])


def spread(value, col, cols):
    got, span = None, 2
    while span < cols:
        new = lax.ppermute(value, "cols", [(i, i + span) for i in range(min(span, cols - span))])
        got = new if got is None else jnp.where(col < span, got, new)
        span *= 2
        if span < cols:
            value = jnp.where(col < 2, value, got)
    return got


def bits_of(size):
    bits, bit = [], 1
    while bit < size:
        bits.append(bit)
        bit *= 2
    return bits


def sum_steps(mine, got, row, rows):
    bits = bits_of(rows)[1:]
    after = yield
    for bit in bits:
        mine, give = halve(mine, got, (row // bit) % 2, after)
        got = swap(give, "rows", rows, bit)
        after = yield mine
    value = add(mine, got, after)
    for bit in reversed(bits):
        got = swap(value, "rows", rows, bit)
        after = yield value
        value = join(value, got, (row // bit) % 2, after)
    yield value


def program(rows_n, cols_n):
    bits = bits_of(rows_n)[1:]

    def on_device(features):
        rows, panels, _, width = features.shape
        halves = width // LANES
        row, col = lax.axis_index("rows"), lax.axis_index("cols")
        side, core, owner = row % 2, col % 2, (col < 2).astype(jnp.int32)
        slabs, own = own_panel(features)
        pieces = [spread(slab, col, cols_n) for slab in slabs]

        other = swap(own, "cols", cols_n, 1)
        gram, give = panel_gram(jnp.stack([side, core]), own, other)
        gram = add(gram, swap(give, "rows", rows_n, 1))
        order = (gram,)
        for bit in bits:
            gram = add(gram, swap(gram, "rows", rows_n, bit))
        gram = join(gram, swap(gram, "rows", rows_n, 1), side)

        flags = jnp.stack([side, core, owner])
        sums, shares = [], []
        for half in range(halves):
            piece = held(pieces[half], *order)
            twin = swap(piece, "cols", cols_n, 1)
            share = [slabs[half], other[half], piece, twin]
            give, keep = panel_products(
                half, flags, features, slabs[half], other, piece, twin, gram)
            order = (give,)
            shares += share
            steps = sum_steps(keep, swap(give, "rows", rows_n, 1), row, rows_n)
            next(steps)
            sums.append(steps)

        lead, trail = sums
        arrived, last = spread(gram, col, cols_n), give
        steps = 2 * len(bits) + 1
        for k in range(steps):
            last = near = lead.send(last)
            if k == 0:
                gram = jnp.where(col < 2, gram, held(arrived, last))
                last = state = first_stage(core, gram, swap(gram, "cols", cols_n, 1), last)
            elif k < STAGES:
                last = state = later_stage(k, state, last)
            if k == steps - 1:
                basis, q_high, q_low = panel_bases(flags, shares, state, near)
                last = q_high
            last = far = trail.send(last)

        mine = [near, far]
        received = [swap(total, "rows", rows_n, 1) for total in mine]
        inverse = state
        outs = finish(side, features, q_high, q_low, inverse, mine, ())
        factor, trailing = finish(1 - side, features, q_high, q_low, inverse, received, outs)
        basis = basis.reshape(rows, halves, 2, LANES).transpose(0, 2, 1, 3).reshape(rows, 2, width)
        return (factor.reshape(2 * width, panels, 1, width), basis, trailing.reshape(features.shape))

    return on_device


def solution(mesh):
    placed = (P("rows", None, "cols", None),)
    return jax.shard_map(
        program(mesh.shape["rows"], mesh.shape["cols"]),
        mesh=mesh,
        in_specs=placed,
        out_specs=(
            P(None, None, "cols", None),
            P("rows", None, None),
            P("rows", None, "cols", None),
        ),
        check_vma=False,
    )
```

```python
import functools

import jax
import jax.numpy as jnp
from jax import lax
from jax.experimental import pallas as pl
from jax.experimental.pallas import tpu as pltpu
from jax.sharding import PartitionSpec as P

HIGHEST = lax.Precision.HIGHEST
LANES = 128
SUB = 8
F32 = jnp.float32
BF16 = jnp.bfloat16


def params():
    return pltpu.CompilerParams(vmem_limit_bytes=48 * 1024 * 1024)


def vmem_spec():
    return pl.BlockSpec(memory_space=pltpu.VMEM)


def smem_spec():
    return pl.BlockSpec(memory_space=pltpu.SMEM)


def split(value):
    high = value.astype(BF16)
    return high, (value - high.astype(F32)).astype(BF16)


NN = (((1,), (0,)), ((), ()))
NT = (((1,), (1,)), ((), ()))


def dot3(left, right, dims=NN):
    def one(a, b):
        return lax.dot_general(a, b, dims, preferred_element_type=F32)

    return one(left[0], right[0]) + (one(left[0], right[1]) + one(left[1], right[0]))


def panel_kernel(x_ref, *refs):
    slabs, both, sems = refs[:-2], refs[-2], refs[-1]
    copies = [
        pltpu.make_async_copy(x_ref.at[:, 0, half], both.at[half], sems.at[half])
        for half in range(len(slabs))
    ]
    for copy in copies:
        copy.start()
    for half, slab in enumerate(slabs):
        copies[half].wait()
        slab[...] = both[half]


def own_panel(features):
    rows, panels, _, width = features.shape
    halves = width // LANES
    slab = jax.ShapeDtypeStruct((rows, LANES), F32)
    *slabs, both = pl.pallas_call(
        panel_kernel,
        in_specs=[pl.BlockSpec(memory_space=pltpu.HBM)],
        out_specs=[vmem_spec()] * (halves + 1),
        out_shape=[slab] * halves + [jax.ShapeDtypeStruct((halves, rows, LANES), F32)],
        scratch_shapes=[pltpu.SemaphoreType.DMA((halves,))],
        compiler_params=params(),
        cost_estimate=cost(2),
        name="own_panel",
    )(features.reshape(rows, panels, halves, LANES))
    return slabs, both


def any_spec():
    return pl.BlockSpec(memory_space=pl.ANY)


def cost(micros=0):
    return pl.CostEstimate(flops=1 + micros * 10 ** 9, bytes_accessed=1, transcendentals=0)


def held_kernel(value_ref, *refs):
    del value_ref, refs


def held(value, *after):
    return pl.pallas_call(
        held_kernel,
        in_specs=[any_spec()] * (1 + len(after)),
        out_specs=any_spec(),
        out_shape=jax.ShapeDtypeStruct(value.shape, value.dtype),
        input_output_aliases={0: 0},
        compiler_params=params(),
        cost_estimate=cost(),
        name="held",
    )(value, *after)


def halve_kernel(flag_ref, mine_ref, got_ref, *refs):
    keep_ref, give_ref = refs[-2:]
    half = keep_ref.shape[0]
    near = pl.multiple_of(flag_ref[0] * half, half)
    far = pl.multiple_of((1 - flag_ref[0]) * half, half)
    give_ref[...] = mine_ref[pl.ds(far, half), :] + got_ref[pl.ds(far, half), :]
    keep_ref[...] = mine_ref[pl.ds(near, half), :] + got_ref[pl.ds(near, half), :]


def halve(mine, got, flag, *after):
    rows, lanes = mine.shape
    half = jax.ShapeDtypeStruct((rows // 2, lanes), F32)
    return pl.pallas_call(
        halve_kernel,
        in_specs=[smem_spec()] + [vmem_spec()] * 2 + [any_spec()] * len(after),
        out_specs=[vmem_spec()] * 2,
        out_shape=[half, half],
        compiler_params=params(),
        cost_estimate=cost(),
        name="halve",
    )(flag.reshape(1), mine, got, *after)


def add_kernel(mine_ref, got_ref, *refs):
    refs[-1][...] = mine_ref[...] + got_ref[...]


def add(mine, got, *after):
    return pl.pallas_call(
        add_kernel,
        in_specs=[vmem_spec()] * 2 + [any_spec()] * len(after),
        out_specs=vmem_spec(),
        out_shape=jax.ShapeDtypeStruct(mine.shape, F32),
        compiler_params=params(),
        cost_estimate=cost(),
        name="add",
    )(mine, got, *after)


def join_kernel(flag_ref, mine_ref, got_ref, *refs):
    out_ref = refs[-1]
    half = mine_ref.shape[0]
    out_ref[pl.ds(pl.multiple_of(flag_ref[0] * half, half), half), :] = mine_ref[...]
    out_ref[pl.ds(pl.multiple_of((1 - flag_ref[0]) * half, half), half), :] = got_ref[...]


def join(mine, got, flag, *after):
    rows, lanes = mine.shape
    return pl.pallas_call(
        join_kernel,
        in_specs=[smem_spec()] + [vmem_spec()] * 2 + [any_spec()] * len(after),
        out_specs=vmem_spec(),
        out_shape=jax.ShapeDtypeStruct((2 * rows, lanes), F32),
        compiler_params=params(),
        cost_estimate=cost(),
        name="join",
    )(flag.reshape(1), mine, got, *after)


def gram_kernel(flags_ref, a_ref, b_ref, keep_ref, give_ref, work_ref):
    flag, core = flags_ref[0], flags_ref[1]

    def pick(zero, one):
        return jnp.where(core == 0, zero, one)

    own = jnp.concatenate([a_ref[0], a_ref[1]], axis=1)
    other = jnp.concatenate([b_ref[0], b_ref[1]], axis=1)
    first = pick(own, other)
    cross = pick(b_ref[0], a_ref[1])
    left = split(jnp.concatenate([own.T, cross.T], axis=0))
    width = own.shape[1]
    mine = dot3(tuple(part[:width] for part in left), split(own))
    mixed = dot3(tuple(part[width:] for part in left), split(first))
    parts = [mine[:LANES, :LANES], mine[LANES:, :LANES], mine[LANES:, LANES:],
             mixed[:, :LANES], mixed[:, LANES:]]
    for i, part in enumerate(parts):
        work_ref[i * LANES:(i + 1) * LANES, :] = part
    half = keep_ref.shape[0]
    keep_ref[...] = work_ref[pl.ds(pl.multiple_of(flag * half, half), half), :]
    give_ref[...] = work_ref[pl.ds(pl.multiple_of((1 - flag) * half, half), half), :]


def panel_gram(flags, own, other):
    half = jax.ShapeDtypeStruct((5 * LANES // 2, LANES), F32)
    return pl.pallas_call(
        gram_kernel,
        in_specs=[smem_spec(), vmem_spec(), vmem_spec()],
        out_specs=[vmem_spec()] * 2,
        out_shape=[half, half],
        scratch_shapes=[pltpu.VMEM((5 * LANES, LANES), F32)],
        compiler_params=params(),
        cost_estimate=cost(1),
        name="panel_gram",
    )(flags, own, other)


def fetch(x_ref, first, slabs_ref, sems):
    copies = []
    for i in range(slabs_ref.shape[0]):
        halves = x_ref.shape[2]
        source = x_ref.at[:, first + i // halves, i % halves]
        copies.append(pltpu.make_async_copy(source, slabs_ref.at[i], sems.at[i]))
    for copy in copies:
        copy.start()
    return copies


def times_columns(left, copies, slabs_ref, out_ref):
    for copy in copies:
        copy.wait()
    right = jnp.concatenate([slabs_ref[i] for i in range(slabs_ref.shape[0])], axis=1)
    value = dot3(left, split(right))
    height = value.shape[0]
    for i in range(slabs_ref.shape[0]):
        out_ref[i * height:(i + 1) * height, :] = value[:, i * LANES:(i + 1) * LANES]


def choose(flags_ref, own, other, got, twin):
    mine = jnp.where(flags_ref[2] == 1, own, got)
    paired = jnp.where(flags_ref[2] == 1, other, twin)
    zero = jnp.where(flags_ref[1] == 0, mine, paired)
    one = jnp.where(flags_ref[1] == 0, paired, mine)
    return zero, one


def product_kernel(flags_ref, x_ref, own_ref, other_ref, got_ref, twin_ref, *refs):
    give_ref, keep_ref, far_ref, near_ref, sems = refs[-5:]
    panels = x_ref.shape[1] // 2
    far = fetch(x_ref, (1 - flags_ref[0]) * panels, far_ref, sems.at[0])
    near = fetch(x_ref, flags_ref[0] * panels, near_ref, sems.at[1])
    zero, one = choose(flags_ref, own_ref[...], other_ref[...], got_ref[...], twin_ref[...])
    left = split(jnp.concatenate([zero, one], axis=1).T)
    times_columns(left, far, far_ref, give_ref)
    times_columns(left, near, near_ref, keep_ref)


def panel_products(flags, features, own, other, got, twin, *after):
    rows, panels, _, width = features.shape
    count = panels * width // LANES // 2
    x = features.reshape(rows, panels, width // LANES, LANES)
    out = jax.ShapeDtypeStruct((count * 2 * LANES, LANES), F32)
    return pl.pallas_call(
        product_kernel,
        in_specs=[smem_spec(), pl.BlockSpec(memory_space=pltpu.HBM)]
        + [vmem_spec()] * 4 + [any_spec()] * len(after),
        out_specs=[vmem_spec()] * 2,
        out_shape=[out, out],
        scratch_shapes=[pltpu.VMEM((count, rows, LANES), F32)] * 2
        + [pltpu.SemaphoreType.DMA((2, count))],
        compiler_params=params(),
        cost_estimate=cost(4),
        name="panel_products",
    )(flags, x, own, other, got, twin, *after)


def lane_copy(value, lane):
    return jnp.broadcast_to(value[:, lane:lane + 1], value.shape)


def row_copy(value, row):
    return jnp.broadcast_to(value[row:row + 1, :], value.shape)


def inverse_factor(block):
    groups = LANES // SUB
    lane = lax.broadcasted_iota(jnp.int32, (SUB, LANES), 1)
    sub = lax.broadcasted_iota(jnp.int32, (SUB, LANES), 0)
    work = [block[SUB * g:SUB * (g + 1), :] for g in range(groups)]
    result = []
    for g in range(groups):
        start = SUB * g
        panel = work[g]
        inside = (lane >= start) & (lane < start + SUB)
        cols = [lane_copy(panel, start + j) for j in range(SUB)]
        c = {(s, j): row_copy(cols[j], s) for j in range(SUB) for s in range(j, SUB)}
        mult, recip, diag = {}, [], []
        for i in range(0, SUB, 2):
            a, b, d = c[i, i], c[i + 1, i], c[i + 1, i + 1]
            det = a * d - b * b
            ra, rdet = 1.0 / a, 1.0 / det
            f = b * ra
            mult[i + 1, i] = f
            rb = a * rdet
            recip += [ra, rb]
            diag += [a, det * ra]
            for s in range(i + 2, SUB):
                mult[s, i] = c[s, i] * ra
                c[s, i + 1] = c[s, i + 1] - f * c[s, i]
                mult[s, i + 1] = c[s, i + 1] * rb
            for s in range(i + 2, SUB):
                for t in range(i + 2, s + 1):
                    c[s, t] = (c[s, t] - mult[s, i] * c[t, i]) - mult[s, i + 1] * c[t, i + 1]
        unit = jnp.where(inside, jnp.where(lane == start + sub, 1.0, 0.0), panel)
        upper = []
        for s in range(SUB):
            row = row_copy(unit, s)
            for i in range(s):
                row = row - mult[s, i] * upper[i]
            upper.append(row)
        scaled = [upper[s] * recip[s] for s in range(SUB)]
        nxt = g + 1
        if nxt < groups:
            old = work[nxt]
            new = jnp.where(inside, 0.0, old)
            v = []
            for j in range(SUB):
                e = lane_copy(old, start + j)
                for i in range(j):
                    e = e - mult[j, i] * v[i]
                v.append(e)
                new = new - e * scaled[j]
            work[nxt] = new
            nxt += 1
        if nxt < groups:
            solved = [None] * SUB
            for s in reversed(range(SUB)):
                row = scaled[s]
                for t in reversed(range(s + 1, SUB)):
                    row = row - mult[t, s] * solved[t]
                solved[s] = row
        for later in range(nxt, groups):
            old = work[later]
            new = jnp.where(inside, 0.0, old)
            for j in range(SUB):
                new = new - lane_copy(old, start + j) * solved[j]
            work[later] = new
        rows, dg = upper[0], diag[0]
        for s in range(1, SUB):
            rows = jnp.where(sub == s, upper[s], rows)
            dg = jnp.where(sub == s, diag[s], dg)
        result.append(jnp.where(lane < start + SUB, rows * lax.rsqrt(dg), 0.0))
    return jnp.concatenate(result, axis=0)


def dot6(a, b, dims=NN):
    return lax.dot_general(a, b, dims, precision=HIGHEST, preferred_element_type=F32)


STAGES = 4


def place(i, j):
    return i * (i + 1) // 2 + j


def stage(k, s):
    m = inverse_factor(s[k, k])
    for j in range(k):
        s[k, j] = dot6(m, s[k, j])
    low = {i: dot6(s[i, k], m, NT) for i in range(k + 1, STAGES)}
    s[k, k] = m
    for i in range(k + 1, STAGES):
        for j in range(k + 1, i + 1):
            s[i, j] = s[i, j] - dot6(low[i], low[j], NT)
        for j in range(k):
            s[i, j] = s[i, j] - dot6(low[i], s[k, j])
        s[i, k] = -dot6(low[i], m)


def first_stage_kernel(core_ref, mine_ref, twin_ref, *refs):
    out_ref = refs[-1]
    zero = jnp.where(core_ref[0] == 0, mine_ref[...], twin_ref[...])
    one = jnp.where(core_ref[0] == 0, twin_ref[...], mine_ref[...])

    def block(value, i):
        return value[i * LANES:(i + 1) * LANES]

    s = {
        (0, 0): block(zero, 0), (1, 0): block(zero, 1), (1, 1): block(zero, 2),
        (2, 0): block(zero, 3), (2, 1): block(zero, 4),
        (2, 2): block(one, 0), (3, 2): block(one, 1), (3, 3): block(one, 2),
        (3, 0): block(one, 3), (3, 1): block(one, 4),
    }
    stage(0, s)
    for (i, j), value in s.items():
        out_ref[place(i, j)] = value


def later_stage_kernel(k, in_ref, *refs):
    s = {(i, j): in_ref[place(i, j)] for i in range(STAGES) for j in range(i + 1)}
    stage(k, s)
    for (i, j), value in s.items():
        refs[-1][place(i, j)] = value


def stage_call(kernel, name, operands, scalars, after):
    return pl.pallas_call(
        kernel,
        in_specs=[smem_spec()] * scalars + [vmem_spec()] * (len(operands) - scalars)
        + [any_spec()] * len(after),
        out_specs=vmem_spec(),
        out_shape=jax.ShapeDtypeStruct((place(STAGES, 0), LANES, LANES), F32),
        compiler_params=params(),
        cost_estimate=cost(),
        name=name,
    )(*operands, *after)


def first_stage(core, mine, twin, *after):
    return stage_call(first_stage_kernel, "factor_0", [core.reshape(1), mine, twin], 1, after)


def later_stage(k, state, *after):
    return stage_call(functools.partial(later_stage_kernel, k), "factor_%d" % k, [state], 0, after)


def packed(ref):
    zero = jnp.zeros((LANES, LANES), F32)
    rows = [
        jnp.concatenate([ref[place(i, j)] if j <= i else zero for j in range(STAGES)], axis=1)
        for i in range(STAGES)
    ]
    return jnp.concatenate(rows, axis=0)


def basis_kernel(flags_ref, *refs):
    halves = (len(refs) - 5) // 4
    x_ref, lines_ref, high_ref, low_ref = refs[4 * halves], *refs[-3:]
    zeros, ones = [], []
    for half in range(halves):
        zero, one = choose(flags_ref, *(ref[...] for ref in refs[4 * half:4 * half + 4]))
        zeros.append(zero)
        ones.append(one)
    rows = zeros[0].shape[0]
    panels = jnp.concatenate(zeros + ones, axis=1)
    q = dot3(split(panels), split(packed(x_ref)), NT)
    high, low = split(q)
    high_ref[...] = high
    low_ref[...] = low
    for panel in range(2):
        for half in range(2):
            k = 2 * panel + half
            lines_ref[pl.ds(2 * half + panel, rows, stride=4), :] = q[:, k * LANES:(k + 1) * LANES]


def panel_bases(flags, slabs, inverse, after):
    rows = slabs[0].shape[0]
    size = STAGES * LANES
    step = 256
    piece = pl.BlockSpec((step, LANES), lambda i: (i, 0))
    wide = pl.BlockSpec((step, size), lambda i: (i, 0))
    return pl.pallas_call(
        basis_kernel,
        grid=(rows // step,),
        in_specs=[smem_spec()] + [piece] * len(slabs) + [vmem_spec(), any_spec()],
        out_specs=[pl.BlockSpec((4 * step, LANES), lambda i: (i, 0)), wide, wide],
        out_shape=[
            jax.ShapeDtypeStruct((4 * rows, LANES), F32),
            jax.ShapeDtypeStruct((rows, size), BF16),
            jax.ShapeDtypeStruct((rows, size), BF16),
        ],
        compiler_params=params(),
        cost_estimate=cost(),
        name="panel_bases",
    )(flags, *slabs, inverse, after)


def trailing_kernel(flags_ref, x_ref, qh_ref, ql_ref, inv_ref, h0_ref, h1_ref, *refs):
    factor_ref, out_ref, q_ref, x_slabs, w_slabs, out_slabs, q_sems, x_sems, w_sems, out_sems = refs[-10:]
    count, rows = x_slabs.shape[0], x_slabs.shape[1]
    halves = x_ref.shape[2]
    first = flags_ref[0] * x_ref.shape[1] // 2
    fetched = [
        pltpu.make_async_copy(ref, q_ref.at[i], q_sems.at[i]) for i, ref in enumerate((qh_ref, ql_ref))
    ]
    for copy in fetched:
        copy.start()
    fetched += fetch(x_ref, first, x_slabs, x_sems)
    columns = []
    for i in range(count):
        at = [(2 * i + p) * LANES for p in range(2)]
        columns.append(jnp.concatenate([ref[a:a + LANES] for a in at for ref in (h0_ref, h1_ref)], axis=0))
    w = dot3(split(packed(inv_ref)), split(jnp.concatenate(columns, axis=1)))
    sent = []
    for i in range(count):
        w_slabs[i] = w[:, i * LANES:(i + 1) * LANES]
        target = factor_ref.at[:, first + i // halves, i % halves]
        sent.append(pltpu.make_async_copy(w_slabs.at[i], target, w_sems.at[i]))
        sent[-1].start()
    right = split(w)
    for copy in fetched:
        copy.wait()
    chunks = out_sems.shape[0]
    step = rows // chunks
    for chunk in range(chunks):
        here = pl.ds(chunk * step, step)
        term = dot3((q_ref[0, here, :], q_ref[1, here, :]), right)
        for i in range(count):
            out_slabs[i, here, :] = x_slabs[i, here, :] - term[:, i * LANES:(i + 1) * LANES]
            target = out_ref.at[here, first + i // halves, i % halves]
            sent.append(pltpu.make_async_copy(out_slabs.at[i, here], target, out_sems.at[chunk, i]))
            sent[-1].start()
    for copy in sent:
        copy.wait()


def finish(side, features, q_high, q_low, inverse, pieces, outs, *after):
    rows, panels, _, width = features.shape
    halves = width // LANES
    size = q_high.shape[1]
    count = panels * halves // 2
    x = features.reshape(rows, panels, halves, LANES)
    hbm = pl.BlockSpec(memory_space=pltpu.HBM)
    chunks = 4
    extra = len(outs)
    return pl.pallas_call(
        trailing_kernel,
        in_specs=[smem_spec(), hbm] + [any_spec()] * 2 + [vmem_spec()] * 3 + [hbm] * extra + [any_spec()] * len(after),
        out_specs=[hbm, hbm],
        out_shape=[
            jax.ShapeDtypeStruct((size, panels, halves, LANES), F32),
            jax.ShapeDtypeStruct(x.shape, F32),
        ],
        scratch_shapes=[
            pltpu.VMEM((2, rows, size), BF16),
            pltpu.VMEM((count, rows, LANES), F32),
            pltpu.VMEM((count, size, LANES), F32),
            pltpu.VMEM((count, rows, LANES), F32),
            pltpu.SemaphoreType.DMA((2,)),
            pltpu.SemaphoreType.DMA((count,)),
            pltpu.SemaphoreType.DMA((count,)),
            pltpu.SemaphoreType.DMA((chunks, count)),
        ],
        input_output_aliases={7 + i: i for i in range(extra)},
        compiler_params=params(),
        cost_estimate=cost(5),
        name="finish",
    )(side.reshape(1), x, q_high, q_low, inverse, *pieces, *outs, *after)


def swap(value, axis, size, bit):
    return lax.ppermute(value, axis, [(i, i ^ bit) for i in range(size)])


def spread(value, col, cols):
    got, span = None, 2
    while span < cols:
        new = lax.ppermute(value, "cols", [(i, i + span) for i in range(min(span, cols - span))])
        got = new if got is None else jnp.where(col < span, got, new)
        span *= 2
        if span < cols:
            value = jnp.where(col < 2, value, got)
    return got


def bits_of(size):
    bits, bit = [], 1
    while bit < size:
        bits.append(bit)
        bit *= 2
    return bits


def sum_steps(mine, got, row, rows):
    bits = bits_of(rows)[1:]
    after = yield
    for bit in bits:
        mine, give = halve(mine, got, (row // bit) % 2, after)
        got = swap(give, "rows", rows, bit)
        after = yield mine
    value = add(mine, got, after)
    for bit in reversed(bits):
        got = swap(value, "rows", rows, bit)
        after = yield value
        value = join(value, got, (row // bit) % 2, after)
    yield value


def program(rows_n, cols_n):
    bits = bits_of(rows_n)[1:]

    def on_device(features):
        rows, panels, _, width = features.shape
        halves = width // LANES
        row, col = lax.axis_index("rows"), lax.axis_index("cols")
        side, core, owner = row % 2, col % 2, (col < 2).astype(jnp.int32)
        slabs, own = own_panel(features)
        pieces = [spread(slab, col, cols_n) for slab in slabs]

        other = swap(own, "cols", cols_n, 1)
        gram, give = panel_gram(jnp.stack([side, core]), own, other)
        gram = add(gram, swap(give, "rows", rows_n, 1))
        order = (gram,)
        for bit in bits:
            gram = add(gram, swap(gram, "rows", rows_n, bit))
        gram = join(gram, swap(gram, "rows", rows_n, 1), side)

        flags = jnp.stack([side, core, owner])
        sums, shares = [], []
        for half in range(halves):
            piece = held(pieces[half], *order)
            twin = swap(piece, "cols", cols_n, 1)
            share = [slabs[half], other[half], piece, twin]
            give, keep = panel_products(flags, features, *share, gram)
            order = (give,)
            shares += share
            steps = sum_steps(keep, swap(give, "rows", rows_n, 1), row, rows_n)
            next(steps)
            sums.append(steps)

        lead, trail = sums
        arrived, last = spread(gram, col, cols_n), give
        steps = 2 * len(bits) + 1
        for k in range(steps):
            last = near = lead.send(last)
            if k == 0:
                gram = jnp.where(col < 2, gram, held(arrived, last))
                last = state = first_stage(core, gram, swap(gram, "cols", cols_n, 1), last)
            elif k < STAGES:
                last = state = later_stage(k, state, last)
            if k == steps - 1:
                basis, q_high, q_low = panel_bases(flags, shares, state, near)
                last = q_high
            last = far = trail.send(last)

        mine = [near, far]
        received = [swap(total, "rows", rows_n, 1) for total in mine]
        inverse = state
        outs = finish(side, features, q_high, q_low, inverse, mine, ())
        factor, trailing = finish(1 - side, features, q_high, q_low, inverse, received, outs)
        basis = basis.reshape(rows, halves, 2, LANES).transpose(0, 2, 1, 3).reshape(rows, 2, width)
        return (factor.reshape(2 * width, panels, 1, width), basis, trailing.reshape(features.shape))

    return on_device


def solution(mesh):
    placed = (P("rows", None, "cols", None),)
    return jax.shard_map(
        program(mesh.shape["rows"], mesh.shape["cols"]),
        mesh=mesh,
        in_specs=placed,
        out_specs=(
            P(None, None, "cols", None),
            P("rows", None, None),
            P("rows", None, "cols", None),
        ),
        check_vma=False,
    )
```
